256 devices in a mesh: seq: 128 (over z, x, y), chan: 2 (over core).
Axes of the slice: x: 4, y: 4, z: 8, core: 2. Of those that a mesh axis runs over, the one named last changes fastest.
Arguments:
- signal: bfloat16 [32768, 512], P('seq', 'chan'), may hold values from -6 to 6
- gating: bfloat16 [32768, 512], P('seq', 'chan'), may hold values from -6 to 6
- cotangent: bfloat16 [32768, 512], P('seq', 'chan'), may hold values from -6 to 6
- decay_rates: float32 [512], P('chan'), may hold values from 3.0517577e-07 to 0.03
- skip_gain: float32 [512], P('chan'), may hold values from 0.5 to 1.5
- first_weight: float32 [33, 64], replicated, may hold values from -1 to 1
- first_bias: float32 [64], replicated, may hold values from -3.140625 to 3.140625
- second_weight: float32 [64, 64], replicated, may hold values from -0.75 to 0.75
- second_bias: float32 [64], replicated, may hold values from -3.140625 to 3.140625
- third_weight: float32 [64, 512], P(None, 'chan'), may hold values from -0.75 to 0.75
Outputs:
- output: bfloat16 [32768, 512], P('seq', 'chan')
- grad_signal: bfloat16 [32768, 512], P('seq', 'chan')
- grad_gating: bfloat16 [32768, 512], P('seq', 'chan')
- grad_skip: float32 [512], P('chan')
- grad_first_weight: float32 [33, 64], replicated
- grad_first_bias: float32 [64], replicated
- grad_second_weight: float32 [64, 64], replicated
- grad_second_bias: float32 [64], replicated
- grad_third_weight: float32 [64, 512], P(None, 'chan')
The draws below stay inside these ranges and needn't reach their ends.
All inputs are finite; a program needn't handle non-finite values.
Results may differ from the reference program's by a relative error of at most 0.001.
Values may be sent and summed in bfloat16 or wider, within the bound.
A program may use at most 128 MiB of HBM per device.

```python
import math
import jax
import jax.numpy as jnp
from jax import lax

CH = 512
FH = 64
BANDS = 16
EMB = 33
TOKENS = 32768


def level_of(stream_key, extent, cuts, low, top_value):
    def one(axis_at, shards_of):
        heights = jax.random.uniform(jax.random.fold_in(jax.random.fold_in(stream_key, 6), axis_at), (shards_of,), jnp.float32, low / len(cuts), top_value / len(cuts))
        return jnp.repeat(jnp.exp(heights), extent[axis_at] // shards_of).reshape((-1,) + (1,) * (len(extent) - axis_at - 1))

    loudness = one(*cuts[0])
    for cut in cuts[1:]:
        loudness = loudness * one(*cut)
    return loudness


def centred(stream_key, dims, width, most, cuts=(), held_as=jnp.bfloat16):
    drawn = jax.random.normal(stream_key, dims, jnp.float32) * width
    if len(cuts) > 0:
        drawn = level_of(stream_key, dims, cuts, -0.22, 0.18) * drawn
    return jnp.clip(drawn, min=-most, max=most).astype(held_as)


def setup_inputs(seed: int = 0) -> dict:
    splits = jax.random.split(jax.random.key(seed), 11)
    signal = centred(splits[0], (TOKENS, CH), 1.0, 6.0, ((0, 128), (1, 2)))
    gating = centred(splits[1], (TOKENS, CH), 1.0, 6.0, ((0, 128), (1, 2)))
    cotangent = centred(splits[2], (TOKENS, CH), 1.0, 6.0, ((0, 128), (1, 2)))
    decay_rates = jnp.clip(jnp.exp(math.log(0.03) - 11.49582 * jax.random.uniform(splits[3], (CH,), jnp.float32) ** level_of(splits[3], (CH,), ((0, 2),), -0.2, 0.2)), 3.0517577442878974e-07, 0.03)
    skip_gain = jnp.clip(0.5 + 1.0 * jax.random.uniform(splits[4], (CH,), jnp.float32) ** level_of(splits[4], (CH,), ((0, 2),), -0.2, 0.2), 0.5, 1.5)
    first_weight = centred(splits[5], (EMB, FH), EMB ** -0.5, 1.0, (), jnp.float32)
    first_bias = jnp.clip(jax.random.uniform(splits[6], (FH,), jnp.float32, -3.140625, 3.140625), -3.140625, 3.140625)
    second_weight = centred(splits[7], (FH, FH), FH ** -0.5, 0.75, (), jnp.float32)
    second_bias = jnp.clip(jax.random.uniform(splits[8], (FH,), jnp.float32, -3.140625, 3.140625), -3.140625, 3.140625)
    third_weight = centred(splits[9], (FH, CH), FH ** -0.5, 0.75, ((1, 2),), jnp.float32)
    return {"signal": signal, "gating": gating, "cotangent": cotangent, "decay_rates": decay_rates, "skip_gain": skip_gain, "first_weight": first_weight, "first_bias": first_bias, "second_weight": second_weight, "second_bias": second_bias, "third_weight": third_weight}


full_turn = 2.0 * math.pi
norm_eps = 1e-06

def embedding(stamps, length):
    freqs = jnp.arange(1, BANDS + 1, dtype=jnp.int32)
    phases = (stamps[:, None] * freqs[None, :] % length).astype(jnp.float32) * (full_turn / length)
    ramp = stamps.astype(jnp.float32)[:, None] / length
    return jnp.concatenate([ramp, jnp.cos(phases), jnp.sin(phases)], axis=1)

def filter_bank(weights_in, stamps, decay_rates, length):
    first_weight, first_bias, second_weight, second_bias, third_weight = weights_in
    embedded = embedding(stamps, length)
    first = jnp.sin(jnp.dot(embedded, first_weight, precision=lax.Precision.HIGHEST, preferred_element_type=jnp.float32) + first_bias)
    second = jnp.sin(jnp.dot(first, second_weight, precision=lax.Precision.HIGHEST, preferred_element_type=jnp.float32) + second_bias)
    raw_filter = jnp.dot(second, third_weight, precision=lax.Precision.HIGHEST, preferred_element_type=jnp.float32)
    return raw_filter * jnp.exp(-stamps.astype(jnp.float32)[:, None] * decay_rates[None, :])

def reference(signal, gating, cotangent, decay_rates, skip_gain, first_weight, first_bias, second_weight, second_bias, third_weight):
    stamps = jnp.arange(TOKENS, dtype=jnp.int32)
    weights_in = (first_weight, first_bias, second_weight, second_bias, third_weight)

    def normalized(weights_now):
        shaped = filter_bank(weights_now, stamps, decay_rates, TOKENS)
        norm_value = jnp.sqrt(lax.optimization_barrier(jnp.sum(shaped * shaped, axis=0)) + norm_eps)
        return shaped / norm_value
    filt, pull_back = jax.vjp(normalized, weights_in)
    values = signal.astype(jnp.float32)
    padded_len = 2 * TOKENS
    signal_spec = jnp.fft.rfft(values, padded_len, axis=0)
    filter_spec = jnp.fft.rfft(filt, padded_len, axis=0)
    conv = jnp.fft.irfft(signal_spec * filter_spec, padded_len, axis=0)[:TOKENS]
    mixed = conv + skip_gain[None, :] * values
    gate_f = gating.astype(jnp.float32)
    cot_f = cotangent.astype(jnp.float32)
    output = (gate_f * mixed).astype(jnp.bfloat16)
    grad_gating = (cot_f * mixed).astype(jnp.bfloat16)
    dmixed = cot_f * gate_f
    dmixed_spec = jnp.fft.rfft(dmixed, padded_len, axis=0)
    corr_in = jnp.fft.irfft(jnp.conj(filter_spec) * dmixed_spec, padded_len, axis=0)[:TOKENS]
    grad_signal = (corr_in + skip_gain[None, :] * dmixed).astype(jnp.bfloat16)
    dfilt = jnp.fft.irfft(jnp.conj(signal_spec) * dmixed_spec, padded_len, axis=0)[:TOKENS]
    grad_skip = lax.optimization_barrier(jnp.sum(dmixed * values, axis=0))
    grads = pull_back(dfilt)[0]
    return (output, grad_signal, grad_gating, grad_skip, grads[0], grads[1], grads[2], grads[3], grads[4])
```

```python
import math

import jax
import jax.numpy as jnp
from jax import lax
from jax.sharding import PartitionSpec as P

BANDS = 16

full_turn = 2.0 * math.pi
norm_eps = 1e-06


def embedding(stamps, length):
    freqs = jnp.arange(1, BANDS + 1, dtype=jnp.int32)
    phases = (stamps[:, None] * freqs[None, :] % length).astype(jnp.float32) * (full_turn / length)
    ramp = stamps.astype(jnp.float32)[:, None] / length
    return jnp.concatenate([ramp, jnp.cos(phases), jnp.sin(phases)], axis=1)


def filter_bank(weights_in, stamps, decay_rates, length):
    first_weight, first_bias, second_weight, second_bias, third_weight = weights_in
    embedded = embedding(stamps, length)
    first = jnp.sin(
        jnp.dot(
            embedded,
            first_weight,
            precision=lax.Precision.HIGHEST,
            preferred_element_type=jnp.float32,
        )
        + first_bias
    )
    second = jnp.sin(
        jnp.dot(
            first,
            second_weight,
            precision=lax.Precision.HIGHEST,
            preferred_element_type=jnp.float32,
        )
        + second_bias
    )
    raw_filter = jnp.dot(
        second, third_weight, precision=lax.Precision.HIGHEST, preferred_element_type=jnp.float32
    )
    return raw_filter * jnp.exp(-stamps.astype(jnp.float32)[:, None] * decay_rates[None, :])


def angles(left_idx, right_idx, period):
    phase = (left_idx[:, None] * right_idx[None, :] % period).astype(jnp.float32) * (
        full_turn / period
    )
    return (jnp.cos(phase), jnp.sin(phase))


def product(form, left_arr, right_arr):
    return jnp.einsum(
        form,
        left_arr,
        right_arr,
        precision=lax.Precision.HIGH,
        preferred_element_type=jnp.float32,
    )


def local_forward(blocks):
    outer_count = blocks.shape[1]
    outer_len = 2 * outer_count
    inner_len = blocks.shape[2]
    padded_len = outer_len * inner_len
    outer_idx = jnp.arange(outer_len, dtype=jnp.int32)
    inner_idx = jnp.arange(inner_len, dtype=jnp.int32)
    cos_outer, sin_outer = angles(outer_idx, jnp.arange(outer_count, dtype=jnp.int32), outer_len)
    part_real = product("ka,cab->ckb", cos_outer, blocks)
    part_imag = -product("ka,cab->ckb", sin_outer, blocks)
    cos_twist, sin_twist = angles(outer_idx, inner_idx, padded_len)
    twist_real = part_real * cos_twist[None] + part_imag * sin_twist[None]
    twist_imag = part_imag * cos_twist[None] - part_real * sin_twist[None]
    cos_inner, sin_inner = angles(inner_idx, inner_idx, inner_len)
    spec_real = product("ckb,bm->ckm", twist_real, cos_inner) + product(
        "ckb,bm->ckm", twist_imag, sin_inner
    )
    spec_imag = product("ckb,bm->ckm", twist_imag, cos_inner) - product(
        "ckb,bm->ckm", twist_real, sin_inner
    )
    return (spec_real, spec_imag)


def local_inverse(spec_real, spec_imag):
    outer_len = spec_real.shape[1]
    outer_count = outer_len // 2
    inner_len = spec_real.shape[2]
    padded_len = outer_len * inner_len
    outer_idx = jnp.arange(outer_len, dtype=jnp.int32)
    inner_idx = jnp.arange(inner_len, dtype=jnp.int32)
    cos_inner, sin_inner = angles(inner_idx, inner_idx, inner_len)
    back_real = product("ckm,mb->ckb", spec_real, cos_inner) - product(
        "ckm,mb->ckb", spec_imag, sin_inner
    )
    back_imag = product("ckm,mb->ckb", spec_imag, cos_inner) + product(
        "ckm,mb->ckb", spec_real, sin_inner
    )
    cos_twist, sin_twist = angles(outer_idx, inner_idx, padded_len)
    twist_real = back_real * cos_twist[None] - back_imag * sin_twist[None]
    twist_imag = back_imag * cos_twist[None] + back_real * sin_twist[None]
    cos_outer, sin_outer = angles(jnp.arange(outer_count, dtype=jnp.int32), outer_idx, outer_len)
    summed = product("ak,ckb->cab", cos_outer, twist_real) - product(
        "ak,ckb->cab", sin_outer, twist_imag
    )
    return summed * (1.0 / padded_len)


def swap(blocks):
    return lax.all_to_all(blocks, "seq", split_axis=0, concat_axis=0, tiled=True)


def body(
    signal,
    gating,
    cotangent,
    decay_rates,
    skip_gain,
    first_weight,
    first_bias,
    second_weight,
    second_bias,
    third_weight,
):
    rows, width = signal.shape
    parts = lax.axis_size("seq")
    me = lax.axis_index("seq")
    length = rows * parts
    share = width // parts
    stamps = me * rows + jnp.arange(rows, dtype=jnp.int32)

    weights_in = (first_weight, first_bias, second_weight, second_bias, third_weight)
    shaped_rows, pull_back = jax.vjp(
        lambda now: filter_bank(now, stamps, decay_rates, length), weights_in
    )
    values = signal.astype(jnp.float32)
    gate_f = gating.astype(jnp.float32)
    cot_f = cotangent.astype(jnp.float32)
    dmixed_rows = cot_f * gate_f

    sent = jnp.stack([values.T, dmixed_rows.T, shaped_rows.T], axis=1)
    got = swap(sent.reshape(parts, share * 3 * rows))
    cols = got.reshape(parts, share, 3, rows).transpose(1, 2, 0, 3)
    sig, dmixed, shaped = cols[:, 0], cols[:, 1], cols[:, 2]

    norm_value = jnp.sqrt(jnp.sum(shaped * shaped, axis=(1, 2)) + norm_eps)[:, None, None]
    filt = shaped / norm_value
    spec_real, spec_imag = local_forward(jnp.concatenate([sig, filt, dmixed], axis=0))
    u_real, h_real, dz_real = spec_real[:share], spec_real[share : 2 * share], spec_real[2 * share :]
    u_imag, h_imag, dz_imag = spec_imag[:share], spec_imag[share : 2 * share], spec_imag[2 * share :]
    prod_real = jnp.concatenate(
        [
            u_real * h_real - u_imag * h_imag,
            h_real * dz_real + h_imag * dz_imag,
            u_real * dz_real + u_imag * dz_imag,
        ],
        axis=0,
    )
    prod_imag = jnp.concatenate(
        [
            u_real * h_imag + u_imag * h_real,
            h_real * dz_imag - h_imag * dz_real,
            u_real * dz_imag - u_imag * dz_real,
        ],
        axis=0,
    )
    results = local_inverse(prod_real, prod_imag)
    conv, corr, dfilt = results[:share], results[share : 2 * share], results[2 * share :]
    dshaped = (dfilt - filt * jnp.sum(filt * dfilt, axis=(1, 2))[:, None, None]) / norm_value
    skip_grad = jnp.sum(dmixed * sig, axis=(1, 2))

    back = jnp.stack([conv, corr, dshaped], axis=1)
    back = back.transpose(2, 0, 1, 3).reshape(parts, share * 3 * rows)
    home = swap(back).reshape(width, 3, rows)
    mixed = home[:, 0].T + skip_gain[None, :] * values
    output = (gate_f * mixed).astype(jnp.bfloat16)
    grad_gating = (cot_f * mixed).astype(jnp.bfloat16)
    grad_signal = (home[:, 1].T + skip_gain[None, :] * dmixed_rows).astype(jnp.bfloat16)
    grads = pull_back(home[:, 2].T)[0]

    third_flat = grads[4].T.reshape(parts, -1)
    shared = jnp.concatenate([g.reshape(-1) for g in grads[:4]])
    count = shared.shape[0]
    piece = -(-count // parts)
    shared = jnp.pad(shared, (0, piece * parts - count)).reshape(parts, piece)
    summed = jnp.sum(swap(jnp.concatenate([third_flat, shared], axis=1)), axis=0)
    third_count = third_flat.shape[1]
    shared_mine = lax.psum(summed[third_count:], "chan")
    mine = jnp.concatenate([summed[:third_count], shared_mine, skip_grad])
    full = swap(jnp.broadcast_to(mine[None], (parts, mine.shape[0])))
    grad_third = full[:, :third_count].reshape(width, -1).T
    shared_full = full[:, third_count : third_count + piece].reshape(-1)
    grad_skip = full[:, third_count + piece :].reshape(-1)
    outs = []
    at = 0
    for g in grads[:4]:
        outs.append(shared_full[at : at + g.size].reshape(g.shape))
        at += g.size
    return (output, grad_signal, grad_gating, grad_skip, *outs, grad_third)


def solution(mesh):
    return jax.shard_map(
        body,
        mesh=mesh,
        in_specs=(
            P("seq", "chan"),
            P("seq", "chan"),
            P("seq", "chan"),
            P("chan"),
            P("chan"),
            P(),
            P(),
            P(),
            P(),
            P(None, "chan"),
        ),
        out_specs=(
            P("seq", "chan"),
            P("seq", "chan"),
            P("seq", "chan"),
            P("chan"),
            P(),
            P(),
            P(),
            P(),
            P(None, "chan"),
        ),
        check_vma=False,
    )
```

```python
import functools
import math

import jax
import jax.experimental.pallas as pl
import jax.experimental.pallas.tpu as pltpu
import jax.numpy as jnp
from jax import lax
from jax.sharding import PartitionSpec as P

BANDS = 16

full_turn = 2.0 * math.pi
norm_eps = 1e-06


def embedding(stamps, length):
    freqs = jnp.arange(1, BANDS + 1, dtype=jnp.int32)
    phases = (stamps[:, None] * freqs[None, :] % length).astype(jnp.float32) * (full_turn / length)
    ramp = stamps.astype(jnp.float32)[:, None] / length
    return jnp.concatenate([ramp, jnp.cos(phases), jnp.sin(phases)], axis=1)


def filter_bank(weights_in, stamps, decay_rates, length):
    first_weight, first_bias, second_weight, second_bias, third_weight = weights_in
    embedded = embedding(stamps, length)
    first = jnp.sin(
        jnp.dot(
            embedded,
            first_weight,
            precision=lax.Precision.HIGHEST,
            preferred_element_type=jnp.float32,
        )
        + first_bias
    )
    second = jnp.sin(
        jnp.dot(
            first,
            second_weight,
            precision=lax.Precision.HIGHEST,
            preferred_element_type=jnp.float32,
        )
        + second_bias
    )
    raw_filter = jnp.dot(
        second, third_weight, precision=lax.Precision.HIGHEST, preferred_element_type=jnp.float32
    )
    return raw_filter * jnp.exp(-stamps.astype(jnp.float32)[:, None] * decay_rates[None, :])


def angles(left_idx, right_idx, period):
    phase = (left_idx[:, None] * right_idx[None, :] % period).astype(jnp.float32) * (
        full_turn / period
    )
    return (jnp.cos(phase), jnp.sin(phase))


def product(form, left_arr, right_arr):
    return jnp.einsum(
        form,
        left_arr,
        right_arr,
        precision=lax.Precision.HIGH,
        preferred_element_type=jnp.float32,
    )


def local_forward(blocks):
    outer_count = blocks.shape[1]
    outer_len = 2 * outer_count
    inner_len = blocks.shape[2]
    padded_len = outer_len * inner_len
    outer_idx = jnp.arange(outer_len, dtype=jnp.int32)
    inner_idx = jnp.arange(inner_len, dtype=jnp.int32)
    cos_outer, sin_outer = angles(outer_idx, jnp.arange(outer_count, dtype=jnp.int32), outer_len)
    part_real = product("ka,cab->ckb", cos_outer, blocks)
    part_imag = -product("ka,cab->ckb", sin_outer, blocks)
    cos_twist, sin_twist = angles(outer_idx, inner_idx, padded_len)
    twist_real = part_real * cos_twist[None] + part_imag * sin_twist[None]
    twist_imag = part_imag * cos_twist[None] - part_real * sin_twist[None]
    cos_inner, sin_inner = angles(inner_idx, inner_idx, inner_len)
    spec_real = product("ckb,bm->ckm", twist_real, cos_inner) + product(
        "ckb,bm->ckm", twist_imag, sin_inner
    )
    spec_imag = product("ckb,bm->ckm", twist_imag, cos_inner) - product(
        "ckb,bm->ckm", twist_real, sin_inner
    )
    return (spec_real, spec_imag)


def local_inverse(spec_real, spec_imag):
    outer_len = spec_real.shape[1]
    outer_count = outer_len // 2
    inner_len = spec_real.shape[2]
    padded_len = outer_len * inner_len
    outer_idx = jnp.arange(outer_len, dtype=jnp.int32)
    inner_idx = jnp.arange(inner_len, dtype=jnp.int32)
    cos_inner, sin_inner = angles(inner_idx, inner_idx, inner_len)
    back_real = product("ckm,mb->ckb", spec_real, cos_inner) - product(
        "ckm,mb->ckb", spec_imag, sin_inner
    )
    back_imag = product("ckm,mb->ckb", spec_imag, cos_inner) + product(
        "ckm,mb->ckb", spec_real, sin_inner
    )
    cos_twist, sin_twist = angles(outer_idx, inner_idx, padded_len)
    twist_real = back_real * cos_twist[None] - back_imag * sin_twist[None]
    twist_imag = back_imag * cos_twist[None] + back_real * sin_twist[None]
    cos_outer, sin_outer = angles(jnp.arange(outer_count, dtype=jnp.int32), outer_idx, outer_len)
    summed = product("ak,ckb->cab", cos_outer, twist_real) - product(
        "ak,ckb->cab", sin_outer, twist_imag
    )
    return summed * (1.0 / padded_len)


def swap_kernel(count, *refs):
    ins, outs = refs[:count], refs[count : 2 * count]
    send_sems, recv_sems = refs[2 * count], refs[2 * count + 1]
    parts = ins[0].shape[0]
    me = lax.axis_index("seq")
    barrier = pltpu.get_barrier_semaphore()

    @pl.loop(1, parts)
    def _(step):
        pl.semaphore_signal(
            barrier,
            inc=1,
            device_id={"seq": lax.rem(me + step, parts)},
            device_id_type=pl.DeviceIdType.MESH,
        )

    pl.semaphore_wait(barrier, parts - 1)

    @pl.loop(1, parts)
    def _(step):
        dst = lax.rem(me + step, parts)
        for at in range(count):
            pltpu.make_async_remote_copy(
                src_ref=ins[at].at[dst],
                dst_ref=outs[at].at[me],
                send_sem=send_sems.at[at],
                recv_sem=recv_sems.at[at],
                device_id={"seq": dst},
                device_id_type=pl.DeviceIdType.MESH,
            ).start()

    for at in range(count):
        pltpu.make_async_copy(ins[at].at[me], outs[at].at[me], recv_sems.at[at]).start()
    for at in range(count):
        pltpu.make_async_copy(outs[at], outs[at], recv_sems.at[at]).wait()
        rest = ins[at].at[pl.ds(0, parts - 1)]
        pltpu.make_async_copy(rest, rest, send_sems.at[at]).wait()


def swap(number, *arrays):
    count = len(arrays)
    vmem = pl.BlockSpec(memory_space=pltpu.VMEM)
    return pl.pallas_call(
        functools.partial(swap_kernel, count),
        out_shape=[jax.ShapeDtypeStruct(a.shape, a.dtype) for a in arrays],
        in_specs=[vmem] * count,
        out_specs=[vmem] * count,
        scratch_shapes=[
            pltpu.SemaphoreType.DMA((count,)),
            pltpu.SemaphoreType.DMA((count,)),
        ],
        compiler_params=pltpu.CompilerParams(
            collective_id=number, has_side_effects=True, vmem_limit_bytes=32 << 20
        ),
        name="swap",
    )(*arrays)


def body(
    signal,
    gating,
    cotangent,
    decay_rates,
    skip_gain,
    first_weight,
    first_bias,
    second_weight,
    second_bias,
    third_weight,
):
    rows, width = signal.shape
    parts = lax.axis_size("seq")
    me = lax.axis_index("seq")
    length = rows * parts
    share = width // parts
    stamps = me * rows + jnp.arange(rows, dtype=jnp.int32)

    weights_in = (first_weight, first_bias, second_weight, second_bias, third_weight)
    shaped_rows, pull_back = jax.vjp(
        lambda now: filter_bank(now, stamps, decay_rates, length), weights_in
    )
    values = signal.astype(jnp.float32)
    gate_f = gating.astype(jnp.float32)
    cot_f = cotangent.astype(jnp.float32)
    dmixed_rows = cot_f * gate_f

    sent_wide = jnp.stack([dmixed_rows.T, shaped_rows.T], axis=1)
    sent_wide = sent_wide.reshape(parts, share * 2 * rows // 128, 128)
    sent_sig = signal.T.reshape(parts, share * rows // 128, 128)
    got_wide, got_sig = swap(0, sent_wide, sent_sig)
    wide = got_wide.reshape(parts, share, 2, rows).transpose(1, 2, 0, 3)
    dmixed, shaped = wide[:, 0], wide[:, 1]
    sig = got_sig.reshape(parts, share, rows).transpose(1, 0, 2).astype(jnp.float32)

    norm_value = jnp.sqrt(jnp.sum(shaped * shaped, axis=(1, 2)) + norm_eps)[:, None, None]
    filt = shaped / norm_value
    spec_real, spec_imag = local_forward(jnp.concatenate([sig, filt, dmixed], axis=0))
    u_real, h_real, dz_real = spec_real[:share], spec_real[share : 2 * share], spec_real[2 * share :]
    u_imag, h_imag, dz_imag = spec_imag[:share], spec_imag[share : 2 * share], spec_imag[2 * share :]
    prod_real = jnp.concatenate(
        [
            u_real * h_real - u_imag * h_imag,
            h_real * dz_real + h_imag * dz_imag,
            u_real * dz_real + u_imag * dz_imag,
        ],
        axis=0,
    )
    prod_imag = jnp.concatenate(
        [
            u_real * h_imag + u_imag * h_real,
            h_real * dz_imag - h_imag * dz_real,
            u_real * dz_imag - u_imag * dz_real,
        ],
        axis=0,
    )
    results = local_inverse(prod_real, prod_imag)
    conv, corr, dfilt = results[:share], results[share : 2 * share], results[2 * share :]
    dshaped = (dfilt - filt * jnp.sum(filt * dfilt, axis=(1, 2))[:, None, None]) / norm_value
    skip_grad = jnp.sum(dmixed * sig, axis=(1, 2))

    back = jnp.stack([conv, corr, dshaped], axis=1)
    back = back.transpose(2, 0, 1, 3).reshape(parts, share * 3 * rows // 128, 128)
    home = swap(1, back)[0].reshape(width, 3, rows)
    mixed = home[:, 0].T + skip_gain[None, :] * values
    output = (gate_f * mixed).astype(jnp.bfloat16)
    grad_gating = (cot_f * mixed).astype(jnp.bfloat16)
    grad_signal = (home[:, 1].T + skip_gain[None, :] * dmixed_rows).astype(jnp.bfloat16)
    grads = pull_back(home[:, 2].T)[0]

    third_flat = grads[4].T.reshape(parts, -1)
    shared = jnp.concatenate([g.reshape(-1) for g in grads[:4]])
    count = shared.shape[0]
    piece = -(-count // parts)
    shared = jnp.pad(shared, (0, piece * parts - count)).reshape(parts, piece)
    third_count = third_flat.shape[1]
    packed = jnp.concatenate([third_flat, shared], axis=1)
    used = packed.shape[1] + share
    room = -(-used // 128) * 128
    packed = jnp.pad(packed, ((0, 0), (0, room - packed.shape[1])))
    summed = jnp.sum(swap(2, packed.reshape(parts, -1, 128))[0], axis=0).reshape(-1)
    shared_mine = lax.psum(summed[third_count : third_count + piece], "chan")
    mine = jnp.concatenate([summed[:third_count], shared_mine, skip_grad])
    mine = jnp.pad(mine, (0, room - used)).reshape(1, -1, 128)
    full = swap(3, jnp.broadcast_to(mine, (parts,) + mine.shape[1:]))[0].reshape(parts, -1)
    grad_third = full[:, :third_count].reshape(width, -1).T
    shared_full = full[:, third_count : third_count + piece].reshape(-1)
    grad_skip = full[:, third_count + piece : used].reshape(-1)
    outs = []
    at = 0
    for g in grads[:4]:
        outs.append(shared_full[at : at + g.size].reshape(g.shape))
        at += g.size
    return (output, grad_signal, grad_gating, grad_skip, *outs, grad_third)


def solution(mesh):
    return jax.shard_map(
        body,
        mesh=mesh,
        in_specs=(
            P("seq", "chan"),
            P("seq", "chan"),
            P("seq", "chan"),
            P("chan"),
            P("chan"),
            P(),
            P(),
            P(),
            P(),
            P(None, "chan"),
        ),
        out_specs=(
            P("seq", "chan"),
            P("seq", "chan"),
            P("seq", "chan"),
            P("chan"),
            P(),
            P(),
            P(),
            P(),
            P(None, "chan"),
        ),
        check_vma=False,
    )
```

```python
import math

import jax
import jax.experimental.pallas as pl
import jax.experimental.pallas.tpu as pltpu
import jax.numpy as jnp
import ml_dtypes
import numpy as np
from jax import lax
from jax.sharding import PartitionSpec as P

BANDS = 16
ROWS = 256
PARTS = 128
HALF = 128
LENGTH = ROWS * PARTS
FULL = 2 * LENGTH
FH = 64
EMB = 33

full_turn = 2.0 * math.pi
norm_eps = 1e-06
MESH = pl.DeviceIdType.MESH
BF = jnp.bfloat16
F32 = jnp.float32


def pieces(table):
    high = table.astype(ml_dtypes.bfloat16)
    low = (table - high.astype(np.float64)).astype(ml_dtypes.bfloat16)
    return high, low


def tables():
    freq = np.arange(HALF) + 0.5
    block = np.arange(PARTS)
    inner = np.arange(ROWS)
    outer_angle = full_turn * ((freq[:, None] * block[None, :]) % 256) / 256
    outer = np.concatenate([np.cos(outer_angle), -np.sin(outer_angle)], axis=0)
    back = outer.T * (2.0 / FULL)
    inner_angle = full_turn * ((inner[:, None] * inner[None, :]) % ROWS) / ROWS
    both = np.concatenate([np.cos(inner_angle), np.sin(inner_angle)], axis=1)
    twist = full_turn * (freq[:, None] * inner[None, :]) / FULL
    return (
        *pieces(outer),
        *pieces(back),
        *pieces(both),
        np.cos(twist).astype(np.float32),
        np.sin(twist).astype(np.float32),
    )


def split(arr):
    high = arr.astype(BF)
    return high, (arr - high.astype(F32)).astype(BF)


def dot(left, right):
    return jnp.dot(left, right, preferred_element_type=F32)


def dot3(left, right):
    return dot(left[0], right[0]) + dot(left[0], right[1]) + dot(left[1], right[0])


def contract(left, right, dims, precision):
    return lax.dot_general(
        left, right, ((dims[:1], dims[1:]), ((), ())), precision=precision, preferred_element_type=F32
    )


def total(arr):
    return jnp.sum(arr, axis=(0, 1), keepdims=True)


def kernel(
    signal,
    gating,
    cotangent,
    decay,
    skip_row,
    skip_all,
    w1,
    b1,
    w2,
    b2,
    w3,
    outer_hi,
    outer_lo,
    back_hi,
    back_lo,
    both_hi,
    both_lo,
    twist_cos,
    twist_sin,
    output,
    grad_signal,
    grad_gating,
    grad_skip,
    grad_w1,
    grad_b1,
    grad_w2,
    grad_b2,
    grad_w3,
    w1s,
    w2s,
    emb,
    firstx,
    second,
    cos1,
    cos2,
    fade,
    wide,
    stage,
    send_a,
    recv_a,
    send_b,
    recv_b,
    send_c,
    recv_c,
    send_d,
    recv_d,
    send_e,
    recv_e,
    mine,
    other,
    send_f,
    recv_f,
    spec,
    vals,
    dfilt,
    send_sems,
    recv_sems,
):
    me = lax.axis_index("seq")
    core = lax.axis_index("chan")
    barrier = pltpu.get_barrier_semaphore()

    @pl.loop(1, PARTS)
    def _(step):
        pl.semaphore_signal(
            barrier, inc=1, device_id={"seq": lax.rem(me + step, PARTS)}, device_id_type=MESH
        )

    pl.semaphore_signal(barrier, inc=1, device_id={"chan": 1 - core}, device_id_type=MESH)

    def spread(src_of, own, recv, at):
        @pl.loop(1, PARTS)
        def _(step):
            dst = lax.rem(me + step, PARTS)
            pltpu.make_async_remote_copy(
                src_ref=src_of(dst),
                dst_ref=recv.at[me],
                send_sem=send_sems.at[at],
                recv_sem=recv_sems.at[at],
                device_id={"seq": dst},
                device_id_type=MESH,
            ).start()

        pltpu.make_async_copy(own, recv.at[me], recv_sems.at[at]).start()

    def arrived(recv, at):
        pltpu.make_async_copy(recv, recv, recv_sems.at[at]).wait()

    def left(recv, at):
        rest = recv.at[pl.ds(0, PARTS - 1)]
        pltpu.make_async_copy(rest, rest, send_sems.at[at]).wait()

    def place(plane, arr):
        for q in range(2):
            for h in range(2):
                stage[:, 2 * q + h, plane * 128 : plane * 128 + 128] = arr[
                    q * 128 : q * 128 + 128, h * 128 : h * 128 + 128
                ]

    def put(plane, q, arr):
        for h in range(2):
            stage[:, 2 * q + h, plane * 128 : plane * 128 + 128] = arr[:, h * 128 : h * 128 + 128]

    def take(plane, q):
        return jnp.concatenate(
            [stage[:, 2 * q + h, plane * 128 : plane * 128 + 128] for h in range(2)], axis=1
        )

    place(0, signal[...].astype(F32).T)
    dmixed_rows = cotangent[...].astype(F32) * gating[...].astype(F32)
    wide[...] = dmixed_rows.T
    high = wide[...].astype(BF).astype(F32)
    place(1, high)
    place(2, wide[...] - high)
    send_a[...] = stage[...].astype(BF)

    stamp = me * ROWS + lax.broadcasted_iota(jnp.int32, (BANDS, ROWS), 1)
    band = lax.broadcasted_iota(jnp.int32, (BANDS, ROWS), 0) + 1
    phase = ((stamp * band) & (LENGTH - 1)).astype(F32) * (full_turn / LENGTH)
    emb[0:16, :] = jnp.cos(phase)
    emb[16:32, :] = jnp.sin(phase)
    line = lax.broadcasted_iota(jnp.int32, (8, ROWS), 0)
    ramp = stamp[0:8].astype(F32)
    emb[32:40, :] = jnp.where(line == 0, ramp / LENGTH, jnp.where(line == 1, 1.0, 0.0))
    w1s[0:32, :] = w1[1:33, :]
    w1s[32:40, :] = jnp.zeros((8, FH), F32)
    w1s[32:33, :] = w1[0:1, :]
    w1s[33:34, :] = b1[...]
    w2s[0:64, :] = w2[...]
    w2s[64:72, :] = jnp.zeros((8, FH), F32)
    w2s[64:65, :] = b2[...]
    pre1 = contract(w1s[...], emb[...], (0, 0), lax.Precision.HIGHEST)
    firstx[0:64, :] = jnp.sin(pre1)
    firstx[64:72, :] = jnp.where(line == 0, 1.0, 0.0)
    cos1[...] = jnp.cos(pre1)
    pre2 = contract(w2s[...], firstx[...], (0, 0), lax.Precision.HIGHEST)
    second[...] = jnp.sin(pre2)
    cos2[...] = jnp.cos(pre2)
    rates = jnp.broadcast_to(decay[...], (ROWS, ROWS)).T
    fade[...] = jnp.exp(-jnp.broadcast_to(ramp[0:1], (ROWS, ROWS)) * rates)
    wide[...] = contract(w3[...], second[...], (0, 0), lax.Precision.HIGHEST) * fade[...]
    high = wide[...].astype(BF).astype(F32)
    place(0, high)
    place(1, wide[...] - high)
    send_b[...] = stage[:, :, 0:256].astype(BF)

    pl.semaphore_wait(barrier, PARTS)
    spread(lambda dst: send_a.at[dst], send_a.at[me], recv_a, 0)
    spread(lambda dst: send_b.at[dst], send_b.at[me], recv_b, 1)

    both = (both_hi, both_lo)

    def forward(slot, parts):
        if len(parts) == 1:
            rows = dot(outer_hi[...], parts[0]) + dot(outer_lo[...], parts[0])
        else:
            rows = dot3((outer_hi[...], outer_lo[...]), parts)
        real, imag = rows[0:HALF], rows[HALF:]
        turned = jnp.concatenate(
            [
                real * twist_cos[...] + imag * twist_sin[...],
                imag * twist_cos[...] - real * twist_sin[...],
            ],
            axis=0,
        )
        out = dot3(split(turned), (both_hi[...], both_lo[...]))
        spec[slot, 0] = out[0:HALF, 0:ROWS] + out[HALF:, ROWS:]
        spec[slot, 1] = out[HALF:, 0:ROWS] - out[0:HALF, ROWS:]

    def inverse(real, imag):
        out = dot3(split(jnp.concatenate([real, imag], axis=0)), (both_hi[...], both_lo[...]))
        mid_real = out[0:HALF, 0:ROWS] - out[HALF:, ROWS:]
        mid_imag = out[HALF:, 0:ROWS] + out[0:HALF, ROWS:]
        turned = jnp.concatenate(
            [
                mid_real * twist_cos[...] - mid_imag * twist_sin[...],
                mid_imag * twist_cos[...] + mid_real * twist_sin[...],
            ],
            axis=0,
        )
        return dot3((back_hi[...], back_lo[...]), split(turned))

    arrived(recv_a, 0)
    stage[...] = recv_a[...].astype(F32)
    skip_grads = []
    for q in range(2):
        sig = take(0, q)
        high, low = take(1, q), take(2, q)
        vals[q] = high + low
        skip_grads.append(total(vals[q] * sig))
        forward(q, (sig.astype(BF),))
        forward(2 + q, (high.astype(BF), low.astype(BF)))
    for q in range(2):
        sig_re, sig_im, dm_re, dm_im = spec[q, 0], spec[q, 1], spec[2 + q, 0], spec[2 + q, 1]
        dfilt[q] = inverse(sig_re * dm_re + sig_im * dm_im, sig_re * dm_im - sig_im * dm_re)

    arrived(recv_b, 1)
    stage[:, :, 0:256] = recv_b[...].astype(F32)
    filters, scales = [], []
    for q in range(2):
        high, low = take(0, q), take(1, q)
        shaped = high + low
        scale = 1.0 / jnp.sqrt(total(shaped * shaped) + norm_eps)
        filt = shaped * scale
        filters.append((high.astype(BF), low.astype(BF)))
        scales.append(scale)
        dfilt[q] = (dfilt[q] - filt * total(filt * dfilt[q])) * scale
    for q in range(2):
        high = dfilt[q].astype(BF).astype(F32)
        put(0, q, high)
        put(1, q, dfilt[q] - high)
    send_c[...] = stage[:, :, 0:256].astype(BF)
    spread(lambda dst: send_c.at[dst], send_c.at[me], recv_c, 2)

    for q in range(2):
        forward(4 + q, filters[q])
    for q in range(2):
        filt_re, filt_im = spec[4 + q, 0] * scales[q], spec[4 + q, 1] * scales[q]
        sig_re, sig_im, dm_re, dm_im = spec[q, 0], spec[q, 1], spec[2 + q, 0], spec[2 + q, 1]
        conv = inverse(sig_re * filt_re - sig_im * filt_im, sig_re * filt_im + sig_im * filt_re)
        high = conv.astype(BF).astype(F32)
        put(0, q, high)
        put(1, q, conv - high)
        corr = inverse(filt_re * dm_re + filt_im * dm_im, filt_re * dm_im - filt_im * dm_re)
        put(2, q, corr + skip_all[me + q * PARTS] * vals[q])
    send_d[...] = stage[...].astype(BF)
    spread(lambda dst: send_d.at[dst], send_d.at[me], recv_d, 3)

    arrived(recv_c, 2)
    stage[:, :, 0:256] = recv_c[...].astype(F32)
    for q in range(2):
        wide[q * 128 : q * 128 + 128, :] = take(0, q) + take(1, q)
    wide[...] = wide[...] * fade[...]
    draw = wide[...]
    third = contract(draw, second[...], (1, 1), lax.Precision.HIGH)
    dpre2 = contract(w3[...], draw, (1, 0), lax.Precision.HIGH) * cos2[...]
    grad2 = contract(firstx[...], dpre2, (1, 1), lax.Precision.HIGH)
    dpre1 = contract(w2[...], dpre2, (1, 0), lax.Precision.HIGH) * cos1[...]
    grad1 = contract(emb[...], dpre1, (1, 1), lax.Precision.HIGH)
    send_e[:, 0, :] = jnp.concatenate([third[0:128], third[128:256]], axis=1)
    shared = jnp.concatenate([grad1, grad2, jnp.zeros((16, FH), F32)], axis=0)
    send_e[:, 1, :] = jnp.concatenate([shared, jnp.zeros((128, FH), F32)], axis=1)
    spread(lambda dst: send_e.at[dst], send_e.at[me], recv_e, 4)
    arrived(recv_e, 4)
    summed = jnp.sum(recv_e[...], axis=0)
    mine[...] = summed
    swap = pltpu.make_async_remote_copy(
        src_ref=mine,
        dst_ref=other,
        send_sem=send_sems.at[5],
        recv_sem=recv_sems.at[5],
        device_id={"chan": 1 - core},
        device_id_type=MESH,
    )
    swap.start()
    swap.wait()
    lane = lax.broadcasted_iota(jnp.int32, (1, 128), 1)
    send_f[0:1, :] = summed[0:1]
    send_f[1:2, :] = jnp.where(
        lane < FH,
        summed[1:2] + other[1:2, :],
        jnp.where(lane == FH, skip_grads[0], skip_grads[1]),
    )
    spread(lambda dst: send_f, send_f, recv_f, 6)

    arrived(recv_d, 3)
    stage[...] = recv_d[...].astype(F32)
    for q in range(2):
        wide[q * 128 : q * 128 + 128, :] = take(0, q) + take(1, q)
    mixed = wide[...].T + skip_row[...] * signal[...].astype(F32)
    output[...] = (gating[...].astype(F32) * mixed).astype(BF)
    grad_gating[...] = (cotangent[...].astype(F32) * mixed).astype(BF)
    for q in range(2):
        wide[q * 128 : q * 128 + 128, :] = take(2, q)
    grad_signal[...] = wide[...].T.astype(BF)

    arrived(recv_f, 6)
    thirds = recv_f[:, 0, :].T
    grad_w3[:, 0:128] = thirds[0:64]
    grad_w3[:, 128:256] = thirds[64:128]
    rest = recv_f[:, 1, :]
    skips = rest.T
    grad_skip[:, 0:128] = skips[64:65]
    grad_skip[:, 128:256] = skips[65:66]
    grad_w1[1:33, :] = rest[0:32, 0:64]
    grad_w1[0:1, :] = rest[32:33, 0:64]
    grad_b1[...] = rest[33:34, 0:64]
    grad_w2[...] = rest[40:104, 0:64]
    grad_b2[...] = rest[104:105, 0:64]

    left(send_a, 0)
    left(send_b, 1)
    left(send_c, 2)
    left(send_d, 3)
    left(send_e, 4)
    left(recv_f, 6)


def body(
    signal,
    gating,
    cotangent,
    decay_rates,
    skip_gain,
    first_weight,
    first_bias,
    second_weight,
    second_bias,
    third_weight,
):
    vmem = pl.BlockSpec(memory_space=pltpu.VMEM)
    smem = pl.BlockSpec(memory_space=pltpu.SMEM)
    consts = [jnp.asarray(t) for t in tables()]
    wide_msg = pltpu.VMEM((PARTS, 4, 384), BF)
    thin_msg = pltpu.VMEM((PARTS, 4, 256), BF)
    pair = pltpu.VMEM((2, 128), F32)
    results = pl.pallas_call(
        kernel,
        out_shape=[
            jax.ShapeDtypeStruct((ROWS, ROWS), BF),
            jax.ShapeDtypeStruct((ROWS, ROWS), BF),
            jax.ShapeDtypeStruct((ROWS, ROWS), BF),
            jax.ShapeDtypeStruct((1, ROWS), F32),
            jax.ShapeDtypeStruct((EMB, FH), F32),
            jax.ShapeDtypeStruct((1, FH), F32),
            jax.ShapeDtypeStruct((FH, FH), F32),
            jax.ShapeDtypeStruct((1, FH), F32),
            jax.ShapeDtypeStruct((FH, ROWS), F32),
        ],
        in_specs=[vmem] * 5 + [smem] + [vmem] * 13,
        out_specs=[vmem] * 9,
        scratch_shapes=[
            pltpu.VMEM((40, FH), F32),
            pltpu.VMEM((72, FH), F32),
            pltpu.VMEM((40, ROWS), F32),
            pltpu.VMEM((72, ROWS), F32),
            pltpu.VMEM((FH, ROWS), F32),
            pltpu.VMEM((FH, ROWS), F32),
            pltpu.VMEM((FH, ROWS), F32),
            pltpu.VMEM((ROWS, ROWS), F32),
            pltpu.VMEM((ROWS, ROWS), F32),
            pltpu.VMEM((PARTS, 4, 384), F32),
            wide_msg,
            wide_msg,
            thin_msg,
            thin_msg,
            thin_msg,
            thin_msg,
            wide_msg,
            wide_msg,
            pltpu.VMEM((PARTS, 2, 128), F32),
            pltpu.VMEM((PARTS, 2, 128), F32),
            pair,
            pair,
            pair,
            pltpu.VMEM((PARTS, 2, 128), F32),
            pltpu.VMEM((6, 2, HALF, ROWS), F32),
            pltpu.VMEM((2, PARTS, ROWS), F32),
            pltpu.VMEM((2, PARTS, ROWS), F32),
            pltpu.SemaphoreType.DMA((7,)),
            pltpu.SemaphoreType.DMA((7,)),
        ],
        compiler_params=pltpu.CompilerParams(
            collective_id=0, has_side_effects=True, vmem_limit_bytes=48 << 20
        ),
        name="hyena",
    )(
        signal,
        gating,
        cotangent,
        decay_rates.reshape(1, ROWS),
        skip_gain.reshape(1, ROWS),
        skip_gain,
        first_weight,
        first_bias.reshape(1, FH),
        second_weight,
        second_bias.reshape(1, FH),
        third_weight,
        *consts,
    )
    out, g_sig, g_gate, g_skip, g_w1, g_b1, g_w2, g_b2, g_w3 = results
    return (
        out,
        g_sig,
        g_gate,
        g_skip.reshape(ROWS),
        g_w1,
        g_b1.reshape(FH),
        g_w2,
        g_b2.reshape(FH),
        g_w3,
    )


def solution(mesh):
    return jax.shard_map(
        body,
        mesh=mesh,
        in_specs=(
            P("seq", "chan"),
            P("seq", "chan"),
            P("seq", "chan"),
            P("chan"),
            P("chan"),
            P(),
            P(),
            P(),
            P(),
            P(None, "chan"),
        ),
        out_specs=(
            P("seq", "chan"),
            P("seq", "chan"),
            P("seq", "chan"),
            P("chan"),
            P(),
            P(),
            P(),
            P(),
            P(None, "chan"),
        ),
        check_vma=False,
    )
```

```python
import math

import jax
import jax.experimental.pallas as pl
import jax.experimental.pallas.tpu as pltpu
import jax.numpy as jnp
import ml_dtypes
import numpy as np
from jax import lax
from jax.sharding import PartitionSpec as P

BANDS = 16
ROWS = 256
PARTS = 128
HALF = 128
LENGTH = ROWS * PARTS
FULL = 2 * LENGTH
LIMIT = 64 << 20
FH = 64
EMB = 33

full_turn = 2.0 * math.pi
norm_eps = 1e-06
MESH = pl.DeviceIdType.MESH
BF = jnp.bfloat16
F32 = jnp.float32


def pieces(table):
    high = table.astype(ml_dtypes.bfloat16)
    low = (table - high.astype(np.float64)).astype(ml_dtypes.bfloat16)
    return high, low


def tables():
    freq = np.arange(HALF) + 0.5
    block = np.arange(PARTS)
    inner = np.arange(ROWS)
    outer_angle = full_turn * ((freq[:, None] * block[None, :]) % 256) / 256
    outer = np.concatenate([np.cos(outer_angle), -np.sin(outer_angle)], axis=0)
    back = outer.T * (2.0 / FULL)
    inner_angle = full_turn * ((inner[:, None] * inner[None, :]) % ROWS) / ROWS
    both = np.concatenate([np.cos(inner_angle), np.sin(inner_angle)], axis=1)
    twist = full_turn * (freq[:, None] * inner[None, :]) / FULL
    return (
        *pieces(outer),
        *pieces(back),
        *pieces(both),
        np.cos(twist).astype(np.float32),
        np.sin(twist).astype(np.float32),
    )


def split(arr):
    high = arr.astype(BF)
    return high, (arr - high.astype(F32)).astype(BF)


def dot(left, right):
    return jnp.dot(left, right, preferred_element_type=F32)


def dot3(left, right):
    return dot(left[0], right[0]) + dot(left[0], right[1]) + dot(left[1], right[0])


def contract(left, right, dims, precision):
    return lax.dot_general(
        left, right, ((dims[:1], dims[1:]), ((), ())), precision=precision, preferred_element_type=F32
    )


def total(arr):
    return jnp.sum(arr, axis=(0, 1), keepdims=True)


def deliver(*refs):
    count = len(refs) // 3
    heard, told = refs[-2:]
    ins, outs, held = refs[:count], refs[count : 2 * count], refs[2 * count : 3 * count]
    loads = [pltpu.make_async_copy(ins[at], held[at], heard.at[at]) for at in range(count)]
    stores = [pltpu.make_async_copy(held[at], outs[at], told.at[at]) for at in range(count)]
    for load in loads:
        load.start()
    for load, store in zip(loads, stores):
        load.wait()
        store.start()
    for store in stores:
        store.wait()


def kernel(
    signal_far,
    gating_far,
    cotangent_far,
    decay_far,
    skip_row_far,
    w1_far,
    b1_far,
    w2_far,
    b2_far,
    w3_far,
    outer_hi_far,
    outer_lo_far,
    back_hi_far,
    back_lo_far,
    both_hi_far,
    both_lo_far,
    twist_cos_far,
    twist_sin_far,
    output,
    grad_signal,
    grad_gating,
    grad_skip,
    grad_w1,
    grad_b1,
    grad_w2,
    grad_b2,
    grad_w3,
    signal,
    gating,
    cotangent,
    decay,
    skip_row,
    w1,
    b1,
    w2,
    b2,
    w3,
    outer_hi,
    outer_lo,
    back_hi,
    back_lo,
    both_hi,
    both_lo,
    twist_cos,
    twist_sin,
    load_sems,
    w1s,
    w2s,
    emb,
    firstx,
    second,
    cos1,
    cos2,
    fade,
    wide,
    stage,
    send_a,
    recv_a,
    send_b,
    recv_b,
    send_c,
    recv_c,
    send_d,
    recv_d,
    send_e,
    recv_e,
    mine,
    other,
    send_f,
    recv_f,
    spec,
    vals,
    dfilt,
    send_sems,
    recv_sems,
):
    me = lax.axis_index("seq")
    core = lax.axis_index("chan")
    far = (
        signal_far,
        gating_far,
        cotangent_far,
        decay_far,
        skip_row_far,
        w1_far,
        b1_far,
        w2_far,
        b2_far,
        w3_far,
        outer_hi_far,
        outer_lo_far,
        back_hi_far,
        back_lo_far,
        both_hi_far,
        both_lo_far,
        twist_cos_far,
        twist_sin_far,
    )
    near = (
        signal,
        gating,
        cotangent,
        decay,
        skip_row,
        w1,
        b1,
        w2,
        b2,
        w3,
        outer_hi,
        outer_lo,
        back_hi,
        back_lo,
        both_hi,
        both_lo,
        twist_cos,
        twist_sin,
    )
    loads = [
        pltpu.make_async_copy(far[at], near[at], load_sems.at[at]) for at in range(len(far))
    ]
    for load in loads:
        load.start()
    barrier = pltpu.get_barrier_semaphore()

    @pl.loop(1, PARTS)
    def _(step):
        pl.semaphore_signal(
            barrier, inc=1, device_id={"seq": lax.rem(me + step, PARTS)}, device_id_type=MESH
        )

    pl.semaphore_signal(barrier, inc=1, device_id={"chan": 1 - core}, device_id_type=MESH)

    def spread(src_of, own, recv, at):
        @pl.loop(1, PARTS)
        def _(step):
            dst = lax.rem(me + step, PARTS)
            pltpu.make_async_remote_copy(
                src_ref=src_of(dst),
                dst_ref=recv.at[me],
                send_sem=send_sems.at[at],
                recv_sem=recv_sems.at[at],
                device_id={"seq": dst},
                device_id_type=MESH,
            ).start()

        pltpu.make_async_copy(own, recv.at[me], recv_sems.at[at]).start()

    def arrived(recv, at):
        pltpu.make_async_copy(recv, recv, recv_sems.at[at]).wait()

    def left(recv, at):
        rest = recv.at[pl.ds(0, PARTS - 1)]
        pltpu.make_async_copy(rest, rest, send_sems.at[at]).wait()

    def place(plane, arr):
        for q in range(2):
            for h in range(2):
                stage[:, 2 * q + h, plane * 128 : plane * 128 + 128] = arr[
                    q * 128 : q * 128 + 128, h * 128 : h * 128 + 128
                ]

    def put(plane, q, arr):
        for h in range(2):
            stage[:, 2 * q + h, plane * 128 : plane * 128 + 128] = arr[:, h * 128 : h * 128 + 128]

    def take(plane, q):
        return jnp.concatenate(
            [stage[:, 2 * q + h, plane * 128 : plane * 128 + 128] for h in range(2)], axis=1
        )

    for load in loads:
        load.wait()

    place(0, signal[...].astype(F32).T)
    dmixed_rows = cotangent[...].astype(F32) * gating[...].astype(F32)
    wide[...] = dmixed_rows.T
    high = wide[...].astype(BF).astype(F32)
    place(1, high)
    place(2, wide[...] - high)
    send_a[...] = stage[...].astype(BF)

    stamp = me * ROWS + lax.broadcasted_iota(jnp.int32, (BANDS, ROWS), 1)
    band = lax.broadcasted_iota(jnp.int32, (BANDS, ROWS), 0) + 1
    phase = ((stamp * band) & (LENGTH - 1)).astype(F32) * (full_turn / LENGTH)
    emb[0:16, :] = jnp.cos(phase)
    emb[16:32, :] = jnp.sin(phase)
    line = lax.broadcasted_iota(jnp.int32, (8, ROWS), 0)
    ramp = stamp[0:8].astype(F32)
    emb[32:40, :] = jnp.where(line == 0, ramp / LENGTH, jnp.where(line == 1, 1.0, 0.0))
    w1s[0:32, :] = w1[1:33, :]
    w1s[32:40, :] = jnp.zeros((8, FH), F32)
    w1s[32:33, :] = w1[0:1, :]
    w1s[33:34, :] = b1[...]
    w2s[0:64, :] = w2[...]
    w2s[64:72, :] = jnp.zeros((8, FH), F32)
    w2s[64:65, :] = b2[...]
    pre1 = contract(w1s[...], emb[...], (0, 0), lax.Precision.HIGHEST)
    firstx[0:64, :] = jnp.sin(pre1)
    firstx[64:72, :] = jnp.where(line == 0, 1.0, 0.0)
    cos1[...] = jnp.cos(pre1)
    pre2 = contract(w2s[...], firstx[...], (0, 0), lax.Precision.HIGHEST)
    second[...] = jnp.sin(pre2)
    cos2[...] = jnp.cos(pre2)
    rates = jnp.broadcast_to(decay[...], (ROWS, ROWS)).T
    fade[...] = jnp.exp(-jnp.broadcast_to(ramp[0:1], (ROWS, ROWS)) * rates)
    wide[...] = contract(w3[...], second[...], (0, 0), lax.Precision.HIGHEST) * fade[...]
    high = wide[...].astype(BF).astype(F32)
    place(0, high)
    place(1, wide[...] - high)
    send_b[...] = stage[:, :, 0:256].astype(BF)

    pl.semaphore_wait(barrier, PARTS)
    spread(lambda dst: send_a.at[dst], send_a.at[me], recv_a, 0)
    spread(lambda dst: send_b.at[dst], send_b.at[me], recv_b, 1)

    both = (both_hi, both_lo)

    def forward(slot, parts):
        if len(parts) == 1:
            rows = dot(outer_hi[...], parts[0]) + dot(outer_lo[...], parts[0])
        else:
            rows = dot3((outer_hi[...], outer_lo[...]), parts)
        real, imag = rows[0:HALF], rows[HALF:]
        turned = jnp.concatenate(
            [
                real * twist_cos[...] + imag * twist_sin[...],
                imag * twist_cos[...] - real * twist_sin[...],
            ],
            axis=0,
        )
        out = dot3(split(turned), (both_hi[...], both_lo[...]))
        spec[slot, 0] = out[0:HALF, 0:ROWS] + out[HALF:, ROWS:]
        spec[slot, 1] = out[HALF:, 0:ROWS] - out[0:HALF, ROWS:]

    def inverse(real, imag):
        out = dot3(split(jnp.concatenate([real, imag], axis=0)), (both_hi[...], both_lo[...]))
        mid_real = out[0:HALF, 0:ROWS] - out[HALF:, ROWS:]
        mid_imag = out[HALF:, 0:ROWS] + out[0:HALF, ROWS:]
        turned = jnp.concatenate(
            [
                mid_real * twist_cos[...] - mid_imag * twist_sin[...],
                mid_imag * twist_cos[...] + mid_real * twist_sin[...],
            ],
            axis=0,
        )
        return dot3((back_hi[...], back_lo[...]), split(turned))

    arrived(recv_a, 0)
    stage[...] = recv_a[...].astype(F32)
    skip_grads = []
    channel = lax.broadcasted_iota(jnp.int32, (1, ROWS), 1)
    skips = [
        total(jnp.where(channel == me + q * PARTS, skip_row[...], 0.0)) for q in range(2)
    ]
    for q in range(2):
        sig = take(0, q)
        high, low = take(1, q), take(2, q)
        vals[q] = high + low
        skip_grads.append(total(vals[q] * sig))
        forward(q, (sig.astype(BF),))
        forward(2 + q, (high.astype(BF), low.astype(BF)))
    for q in range(2):
        sig_re, sig_im, dm_re, dm_im = spec[q, 0], spec[q, 1], spec[2 + q, 0], spec[2 + q, 1]
        dfilt[q] = inverse(sig_re * dm_re + sig_im * dm_im, sig_re * dm_im - sig_im * dm_re)

    arrived(recv_b, 1)
    stage[:, :, 0:256] = recv_b[...].astype(F32)
    filters, scales = [], []
    for q in range(2):
        high, low = take(0, q), take(1, q)
        shaped = high + low
        scale = 1.0 / jnp.sqrt(total(shaped * shaped) + norm_eps)
        filt = shaped * scale
        filters.append((high.astype(BF), low.astype(BF)))
        scales.append(scale)
        dfilt[q] = (dfilt[q] - filt * total(filt * dfilt[q])) * scale
    for q in range(2):
        high = dfilt[q].astype(BF).astype(F32)
        put(0, q, high)
        put(1, q, dfilt[q] - high)
    send_c[...] = stage[:, :, 0:256].astype(BF)
    spread(lambda dst: send_c.at[dst], send_c.at[me], recv_c, 2)

    for q in range(2):
        forward(4 + q, filters[q])
    for q in range(2):
        filt_re, filt_im = spec[4 + q, 0] * scales[q], spec[4 + q, 1] * scales[q]
        sig_re, sig_im, dm_re, dm_im = spec[q, 0], spec[q, 1], spec[2 + q, 0], spec[2 + q, 1]
        conv = inverse(sig_re * filt_re - sig_im * filt_im, sig_re * filt_im + sig_im * filt_re)
        high = conv.astype(BF).astype(F32)
        put(0, q, high)
        put(1, q, conv - high)
        corr = inverse(filt_re * dm_re + filt_im * dm_im, filt_re * dm_im - filt_im * dm_re)
        put(2, q, corr + skips[q] * vals[q])
    send_d[...] = stage[...].astype(BF)
    spread(lambda dst: send_d.at[dst], send_d.at[me], recv_d, 3)

    arrived(recv_c, 2)
    stage[:, :, 0:256] = recv_c[...].astype(F32)
    for q in range(2):
        wide[q * 128 : q * 128 + 128, :] = take(0, q) + take(1, q)
    wide[...] = wide[...] * fade[...]
    draw = wide[...]
    third = contract(draw, second[...], (1, 1), lax.Precision.HIGH)
    dpre2 = contract(w3[...], draw, (1, 0), lax.Precision.HIGH) * cos2[...]
    grad2 = contract(firstx[...], dpre2, (1, 1), lax.Precision.HIGH)
    dpre1 = contract(w2[...], dpre2, (1, 0), lax.Precision.HIGH) * cos1[...]
    grad1 = contract(emb[...], dpre1, (1, 1), lax.Precision.HIGH)
    send_e[:, 0, :] = jnp.concatenate([third[0:128], third[128:256]], axis=1)
    shared = jnp.concatenate([grad1, grad2, jnp.zeros((16, FH), F32)], axis=0)
    send_e[:, 1, :] = jnp.concatenate([shared, jnp.zeros((128, FH), F32)], axis=1)
    spread(lambda dst: send_e.at[dst], send_e.at[me], recv_e, 4)
    arrived(recv_e, 4)
    summed = jnp.sum(recv_e[...], axis=0)
    mine[...] = summed
    swap = pltpu.make_async_remote_copy(
        src_ref=mine,
        dst_ref=other,
        send_sem=send_sems.at[5],
        recv_sem=recv_sems.at[5],
        device_id={"chan": 1 - core},
        device_id_type=MESH,
    )
    swap.start()
    swap.wait()
    lane = lax.broadcasted_iota(jnp.int32, (1, 128), 1)
    send_f[0:1, :] = summed[0:1]
    send_f[1:2, :] = jnp.where(
        lane < FH,
        summed[1:2] + other[1:2, :],
        jnp.where(lane == FH, skip_grads[0], skip_grads[1]),
    )
    spread(lambda dst: send_f, send_f, recv_f, 6)

    arrived(recv_d, 3)
    stage[...] = recv_d[...].astype(F32)
    for q in range(2):
        wide[q * 128 : q * 128 + 128, :] = take(0, q) + take(1, q)
    mixed = wide[...].T + skip_row[...] * signal[...].astype(F32)
    output[...] = (gating[...].astype(F32) * mixed).astype(BF)
    grad_gating[...] = (cotangent[...].astype(F32) * mixed).astype(BF)
    for q in range(2):
        wide[q * 128 : q * 128 + 128, :] = take(2, q)
    grad_signal[...] = wide[...].T.astype(BF)

    arrived(recv_f, 6)
    thirds = recv_f[:, 0, :].T
    grad_w3[:, 0:128] = thirds[0:64]
    grad_w3[:, 128:256] = thirds[64:128]
    rest = recv_f[:, 1, :]
    turned = rest.T
    grad_skip[:, 0:128] = turned[64:65]
    grad_skip[:, 128:256] = turned[65:66]
    grad_w1[1:33, :] = rest[0:32, 0:64]
    grad_w1[0:1, :] = rest[32:33, 0:64]
    grad_b1[...] = rest[33:34, 0:64]
    grad_w2[...] = rest[40:104, 0:64]
    grad_b2[...] = rest[104:105, 0:64]

    left(send_a, 0)
    left(send_b, 1)
    left(send_c, 2)
    left(send_d, 3)
    left(send_e, 4)
    left(recv_f, 6)


def body(
    signal,
    gating,
    cotangent,
    decay_rates,
    skip_gain,
    first_weight,
    first_bias,
    second_weight,
    second_bias,
    third_weight,
):
    vmem = pl.BlockSpec(memory_space=pltpu.VMEM)
    hbm = pl.BlockSpec(memory_space=pltpu.HBM)
    operands = (
        signal,
        gating,
        cotangent,
        decay_rates.reshape(1, ROWS),
        skip_gain.reshape(1, ROWS),
        first_weight,
        first_bias.reshape(1, FH),
        second_weight,
        second_bias.reshape(1, FH),
        third_weight,
        *[jnp.asarray(t) for t in tables()],
    )
    wide_msg = pltpu.VMEM((PARTS, 4, 384), BF)
    thin_msg = pltpu.VMEM((PARTS, 4, 256), BF)
    pair = pltpu.VMEM((2, 128), F32)
    results = pl.pallas_call(
        kernel,
        out_shape=[
            jax.ShapeDtypeStruct((ROWS, ROWS), BF),
            jax.ShapeDtypeStruct((ROWS, ROWS), BF),
            jax.ShapeDtypeStruct((ROWS, ROWS), BF),
            jax.ShapeDtypeStruct((1, ROWS), F32),
            jax.ShapeDtypeStruct((EMB, FH), F32),
            jax.ShapeDtypeStruct((1, FH), F32),
            jax.ShapeDtypeStruct((FH, FH), F32),
            jax.ShapeDtypeStruct((1, FH), F32),
            jax.ShapeDtypeStruct((FH, ROWS), F32),
        ],
        in_specs=[hbm] * 18,
        out_specs=[vmem] * 9,
        scratch_shapes=[pltpu.VMEM(o.shape, o.dtype) for o in operands]
        + [
            pltpu.SemaphoreType.DMA((len(operands),)),
            pltpu.VMEM((40, FH), F32),
            pltpu.VMEM((72, FH), F32),
            pltpu.VMEM((40, ROWS), F32),
            pltpu.VMEM((72, ROWS), F32),
            pltpu.VMEM((FH, ROWS), F32),
            pltpu.VMEM((FH, ROWS), F32),
            pltpu.VMEM((FH, ROWS), F32),
            pltpu.VMEM((ROWS, ROWS), F32),
            pltpu.VMEM((ROWS, ROWS), F32),
            pltpu.VMEM((PARTS, 4, 384), F32),
            wide_msg,
            wide_msg,
            thin_msg,
            thin_msg,
            thin_msg,
            thin_msg,
            wide_msg,
            wide_msg,
            pltpu.VMEM((PARTS, 2, 128), F32),
            pltpu.VMEM((PARTS, 2, 128), F32),
            pair,
            pair,
            pair,
            pltpu.VMEM((PARTS, 2, 128), F32),
            pltpu.VMEM((6, 2, HALF, ROWS), F32),
            pltpu.VMEM((2, PARTS, ROWS), F32),
            pltpu.VMEM((2, PARTS, ROWS), F32),
            pltpu.SemaphoreType.DMA((7,)),
            pltpu.SemaphoreType.DMA((7,)),
        ],
        compiler_params=pltpu.CompilerParams(
            collective_id=0, has_side_effects=True, vmem_limit_bytes=LIMIT
        ),
        name="hyena",
    )(*operands)
    results = pl.pallas_call(
        deliver,
        out_shape=[jax.ShapeDtypeStruct(r.shape, r.dtype) for r in results],
        in_specs=[hbm] * 9,
        out_specs=[hbm] * 9,
        scratch_shapes=[pltpu.VMEM(r.shape, r.dtype) for r in results]
        + [pltpu.SemaphoreType.DMA((9,)), pltpu.SemaphoreType.DMA((9,))],
        compiler_params=pltpu.CompilerParams(vmem_limit_bytes=LIMIT),
        name="deliver",
    )(*results)
    out, g_sig, g_gate, g_skip, g_w1, g_b1, g_w2, g_b2, g_w3 = results
    return (
        out,
        g_sig,
        g_gate,
        g_skip.reshape(ROWS),
        g_w1,
        g_b1.reshape(FH),
        g_w2,
        g_b2.reshape(FH),
        g_w3,
    )


def solution(mesh):
    return jax.shard_map(
        body,
        mesh=mesh,
        in_specs=(
            P("seq", "chan"),
            P("seq", "chan"),
            P("seq", "chan"),
            P("chan"),
            P("chan"),
            P(),
            P(),
            P(),
            P(),
            P(None, "chan"),
        ),
        out_specs=(
            P("seq", "chan"),
            P("seq", "chan"),
            P("seq", "chan"),
            P("chan"),
            P(),
            P(),
            P(),
            P(),
            P(None, "chan"),
        ),
        check_vma=False,
    )
```

```python
import math

import jax
import jax.experimental.pallas as pl
import jax.experimental.pallas.tpu as pltpu
import jax.numpy as jnp
import ml_dtypes
import numpy as np
from jax import lax
from jax.sharding import PartitionSpec as P

BANDS = 16
ROWS = 256
PARTS = 128
HALF = 128
LENGTH = ROWS * PARTS
FULL = 2 * LENGTH
LIMIT = 64 << 20
FH = 64
EMB = 33

full_turn = 2.0 * math.pi
norm_eps = 1e-06
MESH = pl.DeviceIdType.MESH
BF = jnp.bfloat16
F32 = jnp.float32


def pieces(table):
    high = table.astype(ml_dtypes.bfloat16)
    low = (table - high.astype(np.float64)).astype(ml_dtypes.bfloat16)
    return high, low


def tables():
    freq = np.arange(HALF) + 0.5
    block = np.arange(PARTS)
    inner = np.arange(ROWS)
    outer_angle = full_turn * ((freq[:, None] * block[None, :]) % 256) / 256
    outer = np.concatenate([np.cos(outer_angle), -np.sin(outer_angle)], axis=0)
    back = outer.T * (2.0 / FULL)
    inner_angle = full_turn * ((inner[:, None] * inner[None, :]) % ROWS) / ROWS
    both = np.concatenate([np.cos(inner_angle), np.sin(inner_angle)], axis=1)
    twist = full_turn * (freq[:, None] * inner[None, :]) / FULL
    return (
        *pieces(outer),
        *pieces(back),
        *pieces(both),
        np.cos(twist).astype(np.float32),
        np.sin(twist).astype(np.float32),
    )


def split(arr):
    high = arr.astype(BF)
    return high, (arr - high.astype(F32)).astype(BF)


def dot(left, right):
    return jnp.dot(left, right, preferred_element_type=F32)


def dot3(left, right):
    return dot(left[0], right[0]) + dot(left[0], right[1]) + dot(left[1], right[0])


def contract(left, right, dims, precision):
    return lax.dot_general(
        left, right, ((dims[:1], dims[1:]), ((), ())), precision=precision, preferred_element_type=F32
    )


def total(arr):
    return jnp.sum(arr, axis=(0, 1), keepdims=True)


def deliver(*refs):
    count = len(refs) // 3
    heard, told = refs[-2:]
    ins, outs, held = refs[:count], refs[count : 2 * count], refs[2 * count : 3 * count]
    loads = [pltpu.make_async_copy(ins[at], held[at], heard.at[at]) for at in range(count)]
    stores = [pltpu.make_async_copy(held[at], outs[at], told.at[at]) for at in range(count)]
    for load in loads:
        load.start()
    for load, store in zip(loads, stores):
        load.wait()
        store.start()
    for store in stores:
        store.wait()


def kernel(
    signal_far,
    gating_far,
    cotangent_far,
    decay_far,
    skip_row_far,
    w1_far,
    b1_far,
    w2_far,
    b2_far,
    w3_far,
    outer_hi_far,
    outer_lo_far,
    back_hi_far,
    back_lo_far,
    both_hi_far,
    both_lo_far,
    twist_cos_far,
    twist_sin_far,
    output_far,
    grad_signal_far,
    grad_gating_far,
    grad_skip,
    grad_w1,
    grad_b1,
    grad_w2,
    grad_b2,
    grad_w3,
    output,
    grad_signal,
    grad_gating,
    store_sems,
    signal,
    gating,
    cotangent,
    decay,
    skip_row,
    w1,
    b1,
    w2,
    b2,
    w3,
    outer_hi,
    outer_lo,
    back_hi,
    back_lo,
    both_hi,
    both_lo,
    twist_cos,
    twist_sin,
    load_sems,
    w1s,
    w2s,
    emb,
    firstx,
    second,
    cos1,
    cos2,
    fade,
    wide,
    stage,
    send_a,
    recv_a,
    send_b,
    recv_b,
    send_c,
    recv_c,
    send_d,
    recv_d,
    send_e,
    recv_e,
    mid,
    mid_other,
    send_g,
    recv_g,
    send_f,
    recv_f,
    send_s,
    recv_s1,
    recv_s,
    shaped_keep,
    spec,
    vals,
    dfilt,
    send_sems,
    recv_sems,
):
    me = lax.axis_index("seq")
    core = lax.axis_index("chan")
    far = (
        signal_far,
        gating_far,
        cotangent_far,
        decay_far,
        skip_row_far,
        w1_far,
        b1_far,
        w2_far,
        b2_far,
        w3_far,
        outer_hi_far,
        outer_lo_far,
        back_hi_far,
        back_lo_far,
        both_hi_far,
        both_lo_far,
        twist_cos_far,
        twist_sin_far,
    )
    near = (
        signal,
        gating,
        cotangent,
        decay,
        skip_row,
        w1,
        b1,
        w2,
        b2,
        w3,
        outer_hi,
        outer_lo,
        back_hi,
        back_lo,
        both_hi,
        both_lo,
        twist_cos,
        twist_sin,
    )
    loads = [
        pltpu.make_async_copy(far[at], near[at], load_sems.at[at]) for at in range(len(far))
    ]
    for load in loads:
        load.start()
    barrier = pltpu.get_barrier_semaphore()

    depth = me >> 4
    plane_at = me & 15
    mine = (plane_at << 3) + depth

    @pl.loop(1, PARTS)
    def _(step):
        pl.semaphore_signal(
            barrier, inc=1, device_id={"seq": (me + step) & (PARTS - 1)}, device_id_type=MESH
        )

    pl.semaphore_signal(barrier, inc=1, device_id={"chan": 1 - core}, device_id_type=MESH)

    def push(src, dst, at, device):
        pltpu.make_async_remote_copy(
            src_ref=src,
            dst_ref=dst,
            send_sem=send_sems.at[at],
            recv_sem=recv_sems.at[at],
            device_id=device,
            device_id_type=MESH,
        ).start()

    def keep(src, dst, at):
        pltpu.make_async_copy(src, dst, recv_sems.at[at]).start()

    def inward(send, recv, at):
        @pl.loop(1, PARTS)
        def _(step):
            dst = (me + step) & (PARTS - 1)
            push(send.at[((dst & 15) << 3) + (dst >> 4)], recv.at[me], at, {"seq": dst})

        keep(send.at[mine], recv.at[me], at)

    def outward(send, recv, at, first=0, last=PARTS):
        @pl.loop(max(first, 1), last)
        def _(step):
            dst = (me + step) & (PARTS - 1)
            push(send.at[dst], recv.at[mine], at, {"seq": dst})

        if first == 0:
            keep(send.at[me], recv.at[mine], at)

    def over_depth(src_of, dst, at):
        @pl.loop(1, 8)
        def _(step):
            peer = (depth + step) & 7
            push(src_of(peer), dst, at, {"seq": (peer << 4) + plane_at})

        keep(src_of(depth), dst, at)

    def over_plane(src_of, dst, at):
        @pl.loop(1, 16)
        def _(step):
            peer = (plane_at + step) & 15
            push(src_of(peer), dst, at, {"seq": (depth << 4) + peer})

        keep(src_of(plane_at), dst, at)

    def arrived(recv, at):
        pltpu.make_async_copy(recv, recv, recv_sems.at[at]).wait()

    def left(like, at, count=PARTS - 1):
        rest = like.at[pl.ds(0, count)]
        pltpu.make_async_copy(rest, rest, send_sems.at[at]).wait()

    def place(plane, arr):
        for q in range(2):
            for h in range(2):
                stage[:, 2 * q + h, plane * 128 : plane * 128 + 128] = arr[
                    q * 128 : q * 128 + 128, h * 128 : h * 128 + 128
                ]

    def put(plane, q, arr):
        for h in range(2):
            stage[:, 2 * q + h, plane * 128 : plane * 128 + 128] = arr[:, h * 128 : h * 128 + 128]

    def take(plane, q):
        return jnp.concatenate(
            [stage[:, 2 * q + h, plane * 128 : plane * 128 + 128] for h in range(2)], axis=1
        )

    for load in loads[:3]:
        load.wait()

    place(0, signal[...].astype(F32).T)
    dmixed_rows = cotangent[...].astype(F32) * gating[...].astype(F32)
    wide[...] = dmixed_rows.T
    high = wide[...].astype(BF).astype(F32)
    place(1, high)
    place(2, wide[...] - high)
    send_a[...] = stage[...].astype(BF)
    pl.semaphore_wait(barrier, PARTS)
    inward(send_a, recv_a, 0)

    for load in loads[3:]:
        load.wait()
    stamp = me * ROWS + lax.broadcasted_iota(jnp.int32, (BANDS, ROWS), 1)
    band = lax.broadcasted_iota(jnp.int32, (BANDS, ROWS), 0) + 1
    phase = ((stamp * band) & (LENGTH - 1)).astype(F32) * (full_turn / LENGTH)
    emb[0:16, :] = jnp.cos(phase)
    emb[16:32, :] = jnp.sin(phase)
    line = lax.broadcasted_iota(jnp.int32, (8, ROWS), 0)
    ramp = stamp[0:8].astype(F32)
    emb[32:40, :] = jnp.where(line == 0, ramp / LENGTH, jnp.where(line == 1, 1.0, 0.0))
    w1s[0:32, :] = w1[1:33, :]
    w1s[32:40, :] = jnp.zeros((8, FH), F32)
    w1s[32:33, :] = w1[0:1, :]
    w1s[33:34, :] = b1[...]
    w2s[0:64, :] = w2[...]
    w2s[64:72, :] = jnp.zeros((8, FH), F32)
    w2s[64:65, :] = b2[...]
    pre1 = contract(w1s[...], emb[...], (0, 0), lax.Precision.HIGHEST)
    firstx[0:64, :] = jnp.sin(pre1)
    firstx[64:72, :] = jnp.where(line == 0, 1.0, 0.0)
    cos1[...] = jnp.cos(pre1)
    pre2 = contract(w2s[...], firstx[...], (0, 0), lax.Precision.HIGHEST)
    second[...] = jnp.sin(pre2)
    cos2[...] = jnp.cos(pre2)
    rates = jnp.broadcast_to(decay[...], (ROWS, ROWS)).T
    fade[...] = jnp.exp(-jnp.broadcast_to(ramp[0:1], (ROWS, ROWS)) * rates)
    shaped_keep[...] = contract(w3[...], second[...], (0, 0), lax.Precision.HIGHEST) * fade[...]
    high = shaped_keep[...].astype(BF).astype(F32)
    place(0, high)
    place(1, shaped_keep[...] - high)
    send_b[...] = stage[:, :, 0:256].astype(BF)
    inward(send_b, recv_b, 1)

    both = (both_hi, both_lo)

    def forward(slot, parts):
        if len(parts) == 1:
            rows = dot(outer_hi[...], parts[0]) + dot(outer_lo[...], parts[0])
        else:
            rows = dot3((outer_hi[...], outer_lo[...]), parts)
        real, imag = rows[0:HALF], rows[HALF:]
        turned = jnp.concatenate(
            [
                real * twist_cos[...] + imag * twist_sin[...],
                imag * twist_cos[...] - real * twist_sin[...],
            ],
            axis=0,
        )
        out = dot3(split(turned), (both_hi[...], both_lo[...]))
        spec[slot, 0] = out[0:HALF, 0:ROWS] + out[HALF:, ROWS:]
        spec[slot, 1] = out[HALF:, 0:ROWS] - out[0:HALF, ROWS:]

    def inverse(real, imag):
        out = dot3(split(jnp.concatenate([real, imag], axis=0)), (both_hi[...], both_lo[...]))
        mid_real = out[0:HALF, 0:ROWS] - out[HALF:, ROWS:]
        mid_imag = out[HALF:, 0:ROWS] + out[0:HALF, ROWS:]
        turned = jnp.concatenate(
            [
                mid_real * twist_cos[...] - mid_imag * twist_sin[...],
                mid_imag * twist_cos[...] + mid_real * twist_sin[...],
            ],
            axis=0,
        )
        return dot3((back_hi[...], back_lo[...]), split(turned))

    arrived(recv_a, 0)
    stage[...] = recv_a[...].astype(F32)
    skip_grads = []
    channel = lax.broadcasted_iota(jnp.int32, (1, ROWS), 1)
    skips = [
        total(jnp.where(channel == mine + q * PARTS, skip_row[...], 0.0)) for q in range(2)
    ]
    for q in range(2):
        sig = take(0, q)
        high, low = take(1, q), take(2, q)
        vals[q] = high + low
        skip_grads.append(total(vals[q] * sig))
        forward(q, (sig.astype(BF),))
        forward(2 + q, (high.astype(BF), low.astype(BF)))
    for q in range(2):
        sig_re, sig_im, dm_re, dm_im = spec[q, 0], spec[q, 1], spec[2 + q, 0], spec[2 + q, 1]
        dfilt[q] = inverse(sig_re * dm_re + sig_im * dm_im, sig_re * dm_im - sig_im * dm_re)

    for q in range(2):
        high = dfilt[q].astype(BF).astype(F32)
        put(0, q, high)
        put(1, q, dfilt[q] - high)
    send_c[...] = stage[:, :, 0:256].astype(BF)
    outward(send_c, recv_c, 2, 0, 72)

    arrived(recv_b, 1)
    stage[:, :, 0:256] = recv_b[...].astype(F32)
    lane = lax.broadcasted_iota(jnp.int32, (1, 128), 1)
    filters, scales = [], []
    scalars = jnp.zeros((1, 128), F32)
    for q in range(2):
        high, low = take(0, q), take(1, q)
        shaped = high + low
        scale = 1.0 / jnp.sqrt(total(shaped * shaped) + norm_eps)
        pull = total(shaped * scale * dfilt[q]) * scale * scale
        filters.append((high.astype(BF), low.astype(BF)))
        scales.append(scale)
        scalars = jnp.where(lane == 2 * q, scale, jnp.where(lane == 2 * q + 1, pull, scalars))
    send_s[...] = scalars
    over_depth(lambda peer: send_s, recv_s1.at[depth], 7)
    outward(send_c, recv_c, 2, 72, PARTS)

    for q in range(2):
        forward(4 + q, filters[q])
    for q in range(2):
        filt_re, filt_im = spec[4 + q, 0] * scales[q], spec[4 + q, 1] * scales[q]
        sig_re, sig_im, dm_re, dm_im = spec[q, 0], spec[q, 1], spec[2 + q, 0], spec[2 + q, 1]
        conv = inverse(sig_re * filt_re - sig_im * filt_im, sig_re * filt_im + sig_im * filt_re)
        high = conv.astype(BF).astype(F32)
        put(0, q, high)
        put(1, q, conv - high)
        corr = inverse(filt_re * dm_re + filt_im * dm_im, filt_re * dm_im - filt_im * dm_re)
        put(2, q, corr + skips[q] * vals[q])
    send_d[...] = stage[...].astype(BF)
    arrived(recv_s1, 7)
    over_plane(lambda peer: recv_s1, recv_s.at[pl.ds(plane_at * 8, 8)], 8)
    outward(send_d, recv_d, 3, 0, 72)

    arrived(recv_c, 2)
    arrived(recv_s, 8)
    stage[:, :, 0:256] = recv_c[...].astype(F32)
    factors = recv_s[:, 0, :]
    for q in range(2):
        at = pl.ds(q * 128, 128)
        scale, pull = factors[:, 2 * q : 2 * q + 1], factors[:, 2 * q + 1 : 2 * q + 2]
        dshaped = (take(0, q) + take(1, q)) * scale - shaped_keep[at, :] * pull
        wide[at, :] = dshaped * fade[at, :]
    draw = wide[...]
    third = contract(draw, second[...], (1, 1), lax.Precision.HIGH)
    dpre2 = contract(w3[...], draw, (1, 0), lax.Precision.HIGH) * cos2[...]
    grad2 = contract(firstx[...], dpre2, (1, 1), lax.Precision.HIGH)
    dpre1 = contract(w2[...], dpre2, (1, 0), lax.Precision.HIGH) * cos1[...]
    grad1 = contract(emb[...], dpre1, (1, 1), lax.Precision.HIGH)
    send_e[:, 0, :] = jnp.concatenate([third[0:128], third[128:256]], axis=1)
    shared = jnp.concatenate([grad1, grad2, jnp.zeros((16, FH), F32)], axis=0)
    send_e[:, 1, :] = jnp.concatenate([shared, jnp.zeros((128, FH), F32)], axis=1)
    over_plane(lambda peer: send_e.at[pl.ds(peer * 8, 8)], recv_e.at[plane_at], 4)
    outward(send_d, recv_d, 3, 72, PARTS)
    arrived(recv_e, 4)
    part = jnp.sum(recv_e[...], axis=0)
    mid[...] = part
    push(mid, mid_other, 5, {"chan": 1 - core})
    owner = lax.broadcasted_iota(jnp.int32, (8, 2, 128), 0)
    row = lax.broadcasted_iota(jnp.int32, (8, 2, 128), 1)
    column = lax.broadcasted_iota(jnp.int32, (8, 2, 128), 2)
    here = (owner == depth) & (row == 1)
    extra = jnp.where(
        here & (column == FH),
        skip_grads[0][None],
        jnp.where(here & (column == FH + 1), skip_grads[1][None], 0.0),
    )
    arrived(mid_other, 5)
    both_cores = (row == 1) & (column < FH)
    send_g[...] = part + jnp.where(both_cores, mid_other[...], extra)
    over_depth(lambda peer: send_g, recv_g.at[depth], 6)
    arrived(recv_g, 6)
    send_f[...] = jnp.sum(recv_g[...], axis=0)
    over_plane(lambda peer: send_f, recv_f.at[pl.ds(plane_at * 8, 8)], 10)

    arrived(recv_d, 3)
    stage[...] = recv_d[...].astype(F32)
    for q in range(2):
        wide[q * 128 : q * 128 + 128, :] = take(0, q) + take(1, q)
    mixed = wide[...].T + skip_row[...] * signal[...].astype(F32)
    output[...] = (gating[...].astype(F32) * mixed).astype(BF)
    grad_gating[...] = (cotangent[...].astype(F32) * mixed).astype(BF)
    for q in range(2):
        wide[q * 128 : q * 128 + 128, :] = take(2, q)
    grad_signal[...] = wide[...].T.astype(BF)

    stores = [
        pltpu.make_async_copy(output, output_far, store_sems.at[0]),
        pltpu.make_async_copy(grad_signal, grad_signal_far, store_sems.at[1]),
        pltpu.make_async_copy(grad_gating, grad_gating_far, store_sems.at[2]),
    ]
    for store in stores:
        store.start()
    arrived(recv_f, 10)
    thirds = recv_f[:, 0, :].T
    grad_w3[:, 0:128] = thirds[0:64]
    grad_w3[:, 128:256] = thirds[64:128]
    rest = recv_f[:, 1, :]
    turned = rest.T
    grad_skip[:, 0:128] = turned[64:65]
    grad_skip[:, 128:256] = turned[65:66]
    grad_w1[1:33, :] = rest[0:32, 0:64]
    grad_w1[0:1, :] = rest[32:33, 0:64]
    grad_b1[...] = rest[33:34, 0:64]
    grad_w2[...] = rest[40:104, 0:64]
    grad_b2[...] = rest[104:105, 0:64]

    for store in stores:
        store.wait()
    left(send_a, 0)
    left(send_b, 1)
    left(send_c, 2)
    left(send_d, 3)
    left(send_e, 4, 120)
    left(mid, 5, 8)
    left(recv_g, 6, 7)
    left(recv_s1, 7, 7)
    left(recv_s, 8, 120)
    left(recv_f, 10, 120)


def body(
    signal,
    gating,
    cotangent,
    decay_rates,
    skip_gain,
    first_weight,
    first_bias,
    second_weight,
    second_bias,
    third_weight,
):
    vmem = pl.BlockSpec(memory_space=pltpu.VMEM)
    hbm = pl.BlockSpec(memory_space=pltpu.HBM)
    operands = (
        signal,
        gating,
        cotangent,
        decay_rates.reshape(1, ROWS),
        skip_gain.reshape(1, ROWS),
        first_weight,
        first_bias.reshape(1, FH),
        second_weight,
        second_bias.reshape(1, FH),
        third_weight,
        *[jnp.asarray(t) for t in tables()],
    )
    wide_msg = pltpu.VMEM((PARTS, 4, 384), BF)
    thin_msg = pltpu.VMEM((PARTS, 4, 256), BF)
    results = pl.pallas_call(
        kernel,
        out_shape=[
            jax.ShapeDtypeStruct((ROWS, ROWS), BF),
            jax.ShapeDtypeStruct((ROWS, ROWS), BF),
            jax.ShapeDtypeStruct((ROWS, ROWS), BF),
            jax.ShapeDtypeStruct((1, ROWS), F32),
            jax.ShapeDtypeStruct((EMB, FH), F32),
            jax.ShapeDtypeStruct((1, FH), F32),
            jax.ShapeDtypeStruct((FH, FH), F32),
            jax.ShapeDtypeStruct((1, FH), F32),
            jax.ShapeDtypeStruct((FH, ROWS), F32),
        ],
        in_specs=[hbm] * 18,
        out_specs=[hbm] * 3 + [vmem] * 6,
        scratch_shapes=[pltpu.VMEM((ROWS, ROWS), BF)] * 3
        + [pltpu.SemaphoreType.DMA((3,))]
        + [pltpu.VMEM(o.shape, o.dtype) for o in operands]
        + [
            pltpu.SemaphoreType.DMA((len(operands),)),
            pltpu.VMEM((40, FH), F32),
            pltpu.VMEM((72, FH), F32),
            pltpu.VMEM((40, ROWS), F32),
            pltpu.VMEM((72, ROWS), F32),
            pltpu.VMEM((FH, ROWS), F32),
            pltpu.VMEM((FH, ROWS), F32),
            pltpu.VMEM((FH, ROWS), F32),
            pltpu.VMEM((ROWS, ROWS), F32),
            pltpu.VMEM((ROWS, ROWS), F32),
            pltpu.VMEM((PARTS, 4, 384), F32),
            wide_msg,
            wide_msg,
            thin_msg,
            thin_msg,
            thin_msg,
            thin_msg,
            wide_msg,
            wide_msg,
            pltpu.VMEM((PARTS, 2, 128), F32),
            pltpu.VMEM((16, 8, 2, 128), F32),
            pltpu.VMEM((8, 2, 128), F32),
            pltpu.VMEM((8, 2, 128), F32),
            pltpu.VMEM((8, 2, 128), F32),
            pltpu.VMEM((8, 8, 2, 128), F32),
            pltpu.VMEM((8, 2, 128), F32),
            pltpu.VMEM((PARTS, 2, 128), F32),
            pltpu.VMEM((1, 128), F32),
            pltpu.VMEM((8, 1, 128), F32),
            pltpu.VMEM((PARTS, 1, 128), F32),
            pltpu.VMEM((ROWS, ROWS), F32),
            pltpu.VMEM((6, 2, HALF, ROWS), F32),
            pltpu.VMEM((2, PARTS, ROWS), F32),
            pltpu.VMEM((2, PARTS, ROWS), F32),
            pltpu.SemaphoreType.DMA((11,)),
            pltpu.SemaphoreType.DMA((11,)),
        ],
        compiler_params=pltpu.CompilerParams(
            collective_id=0, has_side_effects=True, vmem_limit_bytes=LIMIT
        ),
        name="hyena",
    )(*operands)
    results = pl.pallas_call(
        deliver,
        out_shape=[jax.ShapeDtypeStruct(r.shape, r.dtype) for r in results],
        in_specs=[hbm] * 9,
        out_specs=[hbm] * 9,
        scratch_shapes=[pltpu.VMEM(r.shape, r.dtype) for r in results]
        + [pltpu.SemaphoreType.DMA((9,)), pltpu.SemaphoreType.DMA((9,))],
        compiler_params=pltpu.CompilerParams(vmem_limit_bytes=LIMIT),
        name="deliver",
    )(*results)
    out, g_sig, g_gate, g_skip, g_w1, g_b1, g_w2, g_b2, g_w3 = results
    return (
        out,
        g_sig,
        g_gate,
        g_skip.reshape(ROWS),
        g_w1,
        g_b1.reshape(FH),
        g_w2,
        g_b2.reshape(FH),
        g_w3,
    )


def solution(mesh):
    return jax.shard_map(
        body,
        mesh=mesh,
        in_specs=(
            P("seq", "chan"),
            P("seq", "chan"),
            P("seq", "chan"),
            P("chan"),
            P("chan"),
            P(),
            P(),
            P(),
            P(),
            P(None, "chan"),
        ),
        out_specs=(
            P("seq", "chan"),
            P("seq", "chan"),
            P("seq", "chan"),
            P("chan"),
            P(),
            P(),
            P(),
            P(),
            P(None, "chan"),
        ),
        check_vma=False,
    )
```

```python
import math

import jax
import jax.experimental.pallas as pl
import jax.experimental.pallas.tpu as pltpu
import jax.numpy as jnp
import ml_dtypes
import numpy as np
from jax import lax
from jax.sharding import PartitionSpec as P

BANDS = 16
ROWS = 256
PARTS = 128
HALF = 128
LENGTH = ROWS * PARTS
FULL = 2 * LENGTH
LIMIT = 64 << 20
FH = 64
EMB = 33

full_turn = 2.0 * math.pi
norm_eps = 1e-06
MESH = pl.DeviceIdType.MESH
BF = jnp.bfloat16
F32 = jnp.float32


def pieces(table):
    high = table.astype(ml_dtypes.bfloat16)
    low = (table - high.astype(np.float64)).astype(ml_dtypes.bfloat16)
    return high, low


def tables():
    freq = np.arange(HALF) + 0.5
    block = np.arange(PARTS)
    inner = np.arange(ROWS)
    outer_angle = full_turn * ((freq[:, None] * block[None, :]) % 256) / 256
    outer = np.concatenate([np.cos(outer_angle), -np.sin(outer_angle)], axis=0)
    back = outer.T * (2.0 / FULL)
    inner_angle = full_turn * ((inner[:, None] * inner[None, :]) % ROWS) / ROWS
    both = np.concatenate([np.cos(inner_angle), np.sin(inner_angle)], axis=1)
    twist = full_turn * (freq[:, None] * inner[None, :]) / FULL
    return (
        *pieces(outer),
        *pieces(back),
        *pieces(both),
        np.cos(twist).astype(np.float32),
        np.sin(twist).astype(np.float32),
    )


def split(arr):
    high = arr.astype(BF)
    return high, (arr - high.astype(F32)).astype(BF)


def dot(left, right):
    return jnp.dot(left, right, preferred_element_type=F32)


def dot3(left, right):
    return dot(left[0], right[0]) + dot(left[0], right[1]) + dot(left[1], right[0])


def contract(left, right, dims, precision):
    return lax.dot_general(
        left, right, ((dims[:1], dims[1:]), ((), ())), precision=precision, preferred_element_type=F32
    )


def total(arr):
    return jnp.sum(arr, axis=(0, 1), keepdims=True)


def deliver(*refs):
    count = len(refs) // 3
    heard, told = refs[-2:]
    ins, outs, held = refs[:count], refs[count : 2 * count], refs[2 * count : 3 * count]
    loads = [pltpu.make_async_copy(ins[at], held[at], heard.at[at]) for at in range(count)]
    stores = [pltpu.make_async_copy(held[at], outs[at], told.at[at]) for at in range(count)]
    for load in loads:
        load.start()
    for load, store in zip(loads, stores):
        load.wait()
        store.start()
    for store in stores:
        store.wait()


def kernel(
    signal_far,
    gating_far,
    cotangent_far,
    decay_far,
    skip_row_far,
    w1_far,
    b1_far,
    w2_far,
    b2_far,
    w3_far,
    outer_hi_far,
    outer_lo_far,
    back_hi_far,
    back_lo_far,
    both_hi_far,
    both_lo_far,
    twist_cos_far,
    twist_sin_far,
    output_far,
    grad_signal_far,
    grad_gating_far,
    grad_skip,
    grad_w1,
    grad_b1,
    grad_w2,
    grad_b2,
    grad_w3,
    output,
    grad_signal,
    grad_gating,
    store_sems,
    signal,
    gating,
    cotangent,
    decay,
    skip_row,
    w1,
    b1,
    w2,
    b2,
    w3,
    outer_hi,
    outer_lo,
    back_hi,
    back_lo,
    both_hi,
    both_lo,
    twist_cos,
    twist_sin,
    load_sems,
    w1s,
    w2s,
    emb,
    firstx,
    second,
    cos1,
    cos2,
    fade,
    wide,
    stage,
    send_a,
    recv_a,
    send_b,
    recv_b,
    send_c,
    recv_c,
    send_d,
    recv_d,
    send_e,
    recv_e,
    mid,
    mid_other,
    send_g,
    recv_g,
    send_f,
    recv_f,
    send_s,
    recv_s1,
    recv_s,
    shaped_keep,
    spec,
    vals,
    dfilt,
    send_sems,
    recv_sems,
):
    me = lax.axis_index("seq")
    core = lax.axis_index("chan")
    far = (
        signal_far,
        gating_far,
        cotangent_far,
        decay_far,
        skip_row_far,
        w1_far,
        b1_far,
        w2_far,
        b2_far,
        w3_far,
        outer_hi_far,
        outer_lo_far,
        back_hi_far,
        back_lo_far,
        both_hi_far,
        both_lo_far,
        twist_cos_far,
        twist_sin_far,
    )
    near = (
        signal,
        gating,
        cotangent,
        decay,
        skip_row,
        w1,
        b1,
        w2,
        b2,
        w3,
        outer_hi,
        outer_lo,
        back_hi,
        back_lo,
        both_hi,
        both_lo,
        twist_cos,
        twist_sin,
    )
    loads = [
        pltpu.make_async_copy(far[at], near[at], load_sems.at[at]) for at in range(len(far))
    ]

    depth = me >> 4
    plane_at = me & 15
    mine = (plane_at << 3) + depth
    barrier = pltpu.get_barrier_semaphore()

    far_half, near_half = (4, 3, 5, 2), (6, 1, 7, 0)

    def each(steps, visit):
        for ahead in steps:
            base = ((depth + ahead) & 7) << 4

            @pl.loop(1 if ahead == 0 else 0, 16)
            def _(step):
                visit(base + ((plane_at + (step if ahead == 0 else 10 + step)) & 15))

    def greet(dst):
        pl.semaphore_signal(barrier, inc=1, device_id={"seq": dst}, device_id_type=MESH)

    each(far_half + near_half, greet)
    pl.semaphore_signal(barrier, inc=1, device_id={"chan": 1 - core}, device_id_type=MESH)
    for load in loads:
        load.start()

    def push(src, dst, at, device):
        pltpu.make_async_remote_copy(
            src_ref=src,
            dst_ref=dst,
            send_sem=send_sems.at[at],
            recv_sem=recv_sems.at[at],
            device_id=device,
            device_id_type=MESH,
        ).start()

    def keep(src, dst, at):
        pltpu.make_async_copy(src, dst, recv_sems.at[at]).start()

    def inward(send, recv, at):
        def visit(dst):
            push(send.at[((dst & 15) << 3) + (dst >> 4)], recv.at[me], at, {"seq": dst})

        each(far_half + near_half, visit)
        keep(send.at[mine], recv.at[me], at)

    def outward(send, recv, at, steps):
        each(steps, lambda dst: push(send.at[dst], recv.at[mine], at, {"seq": dst}))
        if 0 in steps:
            keep(send.at[me], recv.at[mine], at)

    def over_depth(src_of, dst, at):
        @pl.loop(1, 8)
        def _(step):
            peer = (depth + step) & 7
            push(src_of(peer), dst, at, {"seq": (peer << 4) + plane_at})

        keep(src_of(depth), dst, at)

    def over_plane(src_of, dst, at):
        @pl.loop(1, 16)
        def _(step):
            peer = (plane_at + step) & 15
            push(src_of(peer), dst, at, {"seq": (depth << 4) + peer})

        keep(src_of(plane_at), dst, at)

    def arrived(recv, at):
        pltpu.make_async_copy(recv, recv, recv_sems.at[at]).wait()

    def left(like, at, count=PARTS - 1):
        rest = like.at[pl.ds(0, count)]
        pltpu.make_async_copy(rest, rest, send_sems.at[at]).wait()

    def place(plane, arr):
        for q in range(2):
            for h in range(2):
                stage[:, 2 * q + h, plane * 128 : plane * 128 + 128] = arr[
                    q * 128 : q * 128 + 128, h * 128 : h * 128 + 128
                ]

    def put(plane, q, arr):
        for h in range(2):
            stage[:, 2 * q + h, plane * 128 : plane * 128 + 128] = arr[:, h * 128 : h * 128 + 128]

    def take(plane, q):
        return jnp.concatenate(
            [stage[:, 2 * q + h, plane * 128 : plane * 128 + 128] for h in range(2)], axis=1
        )

    for load in loads[:3]:
        load.wait()

    place(0, signal[...].astype(F32).T)
    dmixed_rows = cotangent[...].astype(F32) * gating[...].astype(F32)
    wide[...] = dmixed_rows.T
    high = wide[...].astype(BF).astype(F32)
    place(1, high)
    place(2, wide[...] - high)
    send_a[...] = stage[...].astype(BF)
    pl.semaphore_wait(barrier, PARTS)
    inward(send_a, recv_a, 0)

    for load in loads[3:]:
        load.wait()
    stamp = me * ROWS + lax.broadcasted_iota(jnp.int32, (BANDS, ROWS), 1)
    band = lax.broadcasted_iota(jnp.int32, (BANDS, ROWS), 0) + 1
    phase = ((stamp * band) & (LENGTH - 1)).astype(F32) * (full_turn / LENGTH)
    emb[0:16, :] = jnp.cos(phase)
    emb[16:32, :] = jnp.sin(phase)
    line = lax.broadcasted_iota(jnp.int32, (8, ROWS), 0)
    ramp = stamp[0:8].astype(F32)
    emb[32:40, :] = jnp.where(line == 0, ramp / LENGTH, jnp.where(line == 1, 1.0, 0.0))
    w1s[0:32, :] = w1[1:33, :]
    w1s[32:40, :] = jnp.zeros((8, FH), F32)
    w1s[32:33, :] = w1[0:1, :]
    w1s[33:34, :] = b1[...]
    w2s[0:64, :] = w2[...]
    w2s[64:72, :] = jnp.zeros((8, FH), F32)
    w2s[64:65, :] = b2[...]
    pre1 = contract(w1s[...], emb[...], (0, 0), lax.Precision.HIGHEST)
    firstx[0:64, :] = jnp.sin(pre1)
    firstx[64:72, :] = jnp.where(line == 0, 1.0, 0.0)
    cos1[...] = jnp.cos(pre1)
    pre2 = contract(w2s[...], firstx[...], (0, 0), lax.Precision.HIGHEST)
    second[...] = jnp.sin(pre2)
    cos2[...] = jnp.cos(pre2)
    rates = jnp.broadcast_to(decay[...], (ROWS, ROWS)).T
    fade[...] = jnp.exp(-jnp.broadcast_to(ramp[0:1], (ROWS, ROWS)) * rates)
    shaped_keep[...] = contract(w3[...], second[...], (0, 0), lax.Precision.HIGHEST) * fade[...]
    high = shaped_keep[...].astype(BF).astype(F32)
    place(0, high)
    place(1, shaped_keep[...] - high)
    send_b[...] = stage[:, :, 0:256].astype(BF)
    inward(send_b, recv_b, 1)

    both = (both_hi, both_lo)

    def forward(slot, parts):
        if len(parts) == 1:
            rows = dot(outer_hi[...], parts[0]) + dot(outer_lo[...], parts[0])
        else:
            rows = dot3((outer_hi[...], outer_lo[...]), parts)
        real, imag = rows[0:HALF], rows[HALF:]
        turned = jnp.concatenate(
            [
                real * twist_cos[...] + imag * twist_sin[...],
                imag * twist_cos[...] - real * twist_sin[...],
            ],
            axis=0,
        )
        out = dot3(split(turned), (both_hi[...], both_lo[...]))
        spec[slot, 0] = out[0:HALF, 0:ROWS] + out[HALF:, ROWS:]
        spec[slot, 1] = out[HALF:, 0:ROWS] - out[0:HALF, ROWS:]

    def inverse(real, imag):
        out = dot3(split(jnp.concatenate([real, imag], axis=0)), (both_hi[...], both_lo[...]))
        mid_real = out[0:HALF, 0:ROWS] - out[HALF:, ROWS:]
        mid_imag = out[HALF:, 0:ROWS] + out[0:HALF, ROWS:]
        turned = jnp.concatenate(
            [
                mid_real * twist_cos[...] - mid_imag * twist_sin[...],
                mid_imag * twist_cos[...] + mid_real * twist_sin[...],
            ],
            axis=0,
        )
        return dot3((back_hi[...], back_lo[...]), split(turned))

    arrived(recv_a, 0)
    stage[...] = recv_a[...].astype(F32)
    skip_grads = []
    channel = lax.broadcasted_iota(jnp.int32, (1, ROWS), 1)
    skips = [
        total(jnp.where(channel == mine + q * PARTS, skip_row[...], 0.0)) for q in range(2)
    ]
    for q in range(2):
        sig = take(0, q)
        high, low = take(1, q), take(2, q)
        vals[q] = high + low
        skip_grads.append(total(vals[q] * sig))
        forward(q, (sig.astype(BF),))
        forward(2 + q, (high.astype(BF), low.astype(BF)))
    for q in range(2):
        sig_re, sig_im, dm_re, dm_im = spec[q, 0], spec[q, 1], spec[2 + q, 0], spec[2 + q, 1]
        dfilt[q] = inverse(sig_re * dm_re + sig_im * dm_im, sig_re * dm_im - sig_im * dm_re)

    for q in range(2):
        high = dfilt[q].astype(BF).astype(F32)
        put(0, q, high)
        put(1, q, dfilt[q] - high)
    send_c[...] = stage[:, :, 0:256].astype(BF)
    outward(send_c, recv_c, 2, far_half)

    arrived(recv_b, 1)
    stage[:, :, 0:256] = recv_b[...].astype(F32)
    lane = lax.broadcasted_iota(jnp.int32, (1, 128), 1)
    filters, scales = [], []
    scalars = jnp.zeros((1, 128), F32)
    for q in range(2):
        high, low = take(0, q), take(1, q)
        shaped = high + low
        along = total(shaped * dfilt[q])
        scale = 1.0 / jnp.sqrt(total(shaped * shaped) + norm_eps)
        pull = along * scale * scale * scale
        filters.append((high.astype(BF), low.astype(BF)))
        scales.append(scale)
        scalars = jnp.where(lane == 2 * q, scale, jnp.where(lane == 2 * q + 1, pull, scalars))
    send_s[...] = scalars
    over_depth(lambda peer: send_s, recv_s1.at[depth], 7)
    outward(send_c, recv_c, 2, near_half)

    for q in range(2):
        forward(4 + q, filters[q])
    for q in range(2):
        filt_re, filt_im = spec[4 + q, 0] * scales[q], spec[4 + q, 1] * scales[q]
        sig_re, sig_im, dm_re, dm_im = spec[q, 0], spec[q, 1], spec[2 + q, 0], spec[2 + q, 1]
        conv = inverse(sig_re * filt_re - sig_im * filt_im, sig_re * filt_im + sig_im * filt_re)
        high = conv.astype(BF).astype(F32)
        put(0, q, high)
        put(1, q, conv - high)
        corr = inverse(filt_re * dm_re + filt_im * dm_im, filt_re * dm_im - filt_im * dm_re)
        put(2, q, corr + skips[q] * vals[q])
    send_d[...] = stage[...].astype(BF)
    arrived(recv_s1, 7)
    over_plane(lambda peer: recv_s1, recv_s.at[pl.ds(plane_at * 8, 8)], 8)
    outward(send_d, recv_d, 3, far_half)

    arrived(recv_c, 2)
    stage[:, :, 0:256] = recv_c[...].astype(F32)
    for q in range(2):
        at = pl.ds(q * 128, 128)
        wide[at, :] = (take(0, q) + take(1, q)) * fade[at, :]
    shaped_keep[...] = shaped_keep[...] * fade[...]
    arrived(recv_s, 8)
    factors = recv_s[:, 0, :]
    for q in range(2):
        at = pl.ds(q * 128, 128)
        scale, pull = factors[:, 2 * q : 2 * q + 1], factors[:, 2 * q + 1 : 2 * q + 2]
        wide[at, :] = wide[at, :] * scale - shaped_keep[at, :] * pull
    draw = wide[...]
    third = contract(draw, second[...], (1, 1), lax.Precision.HIGH)
    dpre2 = contract(w3[...], draw, (1, 0), lax.Precision.HIGH) * cos2[...]
    grad2 = contract(firstx[...], dpre2, (1, 1), lax.Precision.HIGH)
    dpre1 = contract(w2[...], dpre2, (1, 0), lax.Precision.HIGH) * cos1[...]
    grad1 = contract(emb[...], dpre1, (1, 1), lax.Precision.HIGH)
    send_e[:, 0, :] = jnp.concatenate([third[0:128], third[128:256]], axis=1)
    shared = jnp.concatenate([grad1, grad2, jnp.zeros((16, FH), F32)], axis=0)
    send_e[:, 1, :] = jnp.concatenate([shared, jnp.zeros((128, FH), F32)], axis=1)
    over_plane(lambda peer: send_e.at[pl.ds(peer * 8, 8)], recv_e.at[plane_at], 4)
    outward(send_d, recv_d, 3, near_half)
    arrived(recv_e, 4)
    part = jnp.sum(recv_e[...], axis=0)
    mid[...] = part
    push(mid, mid_other, 5, {"chan": 1 - core})
    owner = lax.broadcasted_iota(jnp.int32, (8, 2, 128), 0)
    row = lax.broadcasted_iota(jnp.int32, (8, 2, 128), 1)
    column = lax.broadcasted_iota(jnp.int32, (8, 2, 128), 2)
    here = (owner == depth) & (row == 1)
    extra = jnp.where(
        here & (column == FH),
        skip_grads[0][None],
        jnp.where(here & (column == FH + 1), skip_grads[1][None], 0.0),
    )
    arrived(mid_other, 5)
    both_cores = (row == 1) & (column < FH)
    send_g[...] = part + jnp.where(both_cores, mid_other[...], extra)
    over_depth(lambda peer: send_g, recv_g.at[depth], 6)
    arrived(recv_g, 6)
    send_f[...] = jnp.sum(recv_g[...], axis=0)
    over_plane(lambda peer: send_f, recv_f.at[pl.ds(plane_at * 8, 8)], 10)

    arrived(recv_d, 3)
    stage[...] = recv_d[...].astype(F32)
    for q in range(2):
        wide[q * 128 : q * 128 + 128, :] = take(0, q) + take(1, q)
    mixed = wide[...].T + skip_row[...] * signal[...].astype(F32)
    output[...] = (gating[...].astype(F32) * mixed).astype(BF)
    grad_gating[...] = (cotangent[...].astype(F32) * mixed).astype(BF)
    for q in range(2):
        wide[q * 128 : q * 128 + 128, :] = take(2, q)
    grad_signal[...] = wide[...].T.astype(BF)

    stores = [
        pltpu.make_async_copy(output, output_far, store_sems.at[0]),
        pltpu.make_async_copy(grad_signal, grad_signal_far, store_sems.at[1]),
        pltpu.make_async_copy(grad_gating, grad_gating_far, store_sems.at[2]),
    ]
    for store in stores:
        store.start()
    arrived(recv_f, 10)
    thirds = recv_f[:, 0, :].T
    grad_w3[:, 0:128] = thirds[0:64]
    grad_w3[:, 128:256] = thirds[64:128]
    rest = recv_f[:, 1, :]
    turned = rest.T
    grad_skip[:, 0:128] = turned[64:65]
    grad_skip[:, 128:256] = turned[65:66]
    grad_w1[1:33, :] = rest[0:32, 0:64]
    grad_w1[0:1, :] = rest[32:33, 0:64]
    grad_b1[...] = rest[33:34, 0:64]
    grad_w2[...] = rest[40:104, 0:64]
    grad_b2[...] = rest[104:105, 0:64]

    for store in stores:
        store.wait()
    left(send_a, 0)
    left(send_b, 1)
    left(send_c, 2)
    left(send_d, 3)
    left(send_e, 4, 120)
    left(mid, 5, 8)
    left(recv_g, 6, 7)
    left(recv_s1, 7, 7)
    left(recv_s, 8, 120)
    left(recv_f, 10, 120)


def body(
    signal,
    gating,
    cotangent,
    decay_rates,
    skip_gain,
    first_weight,
    first_bias,
    second_weight,
    second_bias,
    third_weight,
):
    vmem = pl.BlockSpec(memory_space=pltpu.VMEM)
    hbm = pl.BlockSpec(memory_space=pltpu.HBM)
    operands = (
        signal,
        gating,
        cotangent,
        decay_rates.reshape(1, ROWS),
        skip_gain.reshape(1, ROWS),
        first_weight,
        first_bias.reshape(1, FH),
        second_weight,
        second_bias.reshape(1, FH),
        third_weight,
        *[jnp.asarray(t) for t in tables()],
    )
    wide_msg = pltpu.VMEM((PARTS, 4, 384), BF)
    thin_msg = pltpu.VMEM((PARTS, 4, 256), BF)
    results = pl.pallas_call(
        kernel,
        out_shape=[
            jax.ShapeDtypeStruct((ROWS, ROWS), BF),
            jax.ShapeDtypeStruct((ROWS, ROWS), BF),
            jax.ShapeDtypeStruct((ROWS, ROWS), BF),
            jax.ShapeDtypeStruct((1, ROWS), F32),
            jax.ShapeDtypeStruct((EMB, FH), F32),
            jax.ShapeDtypeStruct((1, FH), F32),
            jax.ShapeDtypeStruct((FH, FH), F32),
            jax.ShapeDtypeStruct((1, FH), F32),
            jax.ShapeDtypeStruct((FH, ROWS), F32),
        ],
        in_specs=[hbm] * 18,
        out_specs=[hbm] * 3 + [vmem] * 6,
        scratch_shapes=[pltpu.VMEM((ROWS, ROWS), BF)] * 3
        + [pltpu.SemaphoreType.DMA((3,))]
        + [pltpu.VMEM(o.shape, o.dtype) for o in operands]
        + [
            pltpu.SemaphoreType.DMA((len(operands),)),
            pltpu.VMEM((40, FH), F32),
            pltpu.VMEM((72, FH), F32),
            pltpu.VMEM((40, ROWS), F32),
            pltpu.VMEM((72, ROWS), F32),
            pltpu.VMEM((FH, ROWS), F32),
            pltpu.VMEM((FH, ROWS), F32),
            pltpu.VMEM((FH, ROWS), F32),
            pltpu.VMEM((ROWS, ROWS), F32),
            pltpu.VMEM((ROWS, ROWS), F32),
            pltpu.VMEM((PARTS, 4, 384), F32),
            wide_msg,
            wide_msg,
            thin_msg,
            thin_msg,
            thin_msg,
            thin_msg,
            wide_msg,
            wide_msg,
            pltpu.VMEM((PARTS, 2, 128), F32),
            pltpu.VMEM((16, 8, 2, 128), F32),
            pltpu.VMEM((8, 2, 128), F32),
            pltpu.VMEM((8, 2, 128), F32),
            pltpu.VMEM((8, 2, 128), F32),
            pltpu.VMEM((8, 8, 2, 128), F32),
            pltpu.VMEM((8, 2, 128), F32),
            pltpu.VMEM((PARTS, 2, 128), F32),
            pltpu.VMEM((1, 128), F32),
            pltpu.VMEM((8, 1, 128), F32),
            pltpu.VMEM((PARTS, 1, 128), F32),
            pltpu.VMEM((ROWS, ROWS), F32),
            pltpu.VMEM((6, 2, HALF, ROWS), F32),
            pltpu.VMEM((2, PARTS, ROWS), F32),
            pltpu.VMEM((2, PARTS, ROWS), F32),
            pltpu.SemaphoreType.DMA((11,)),
            pltpu.SemaphoreType.DMA((11,)),
        ],
        compiler_params=pltpu.CompilerParams(
            collective_id=0, has_side_effects=True, vmem_limit_bytes=LIMIT
        ),
        name="hyena",
    )(*operands)
    results = pl.pallas_call(
        deliver,
        out_shape=[jax.ShapeDtypeStruct(r.shape, r.dtype) for r in results],
        in_specs=[hbm] * 9,
        out_specs=[hbm] * 9,
        scratch_shapes=[pltpu.VMEM(r.shape, r.dtype) for r in results]
        + [pltpu.SemaphoreType.DMA((9,)), pltpu.SemaphoreType.DMA((9,))],
        compiler_params=pltpu.CompilerParams(vmem_limit_bytes=LIMIT),
        name="deliver",
    )(*results)
    out, g_sig, g_gate, g_skip, g_w1, g_b1, g_w2, g_b2, g_w3 = results
    return (
        out,
        g_sig,
        g_gate,
        g_skip.reshape(ROWS),
        g_w1,
        g_b1.reshape(FH),
        g_w2,
        g_b2.reshape(FH),
        g_w3,
    )


def solution(mesh):
    return jax.shard_map(
        body,
        mesh=mesh,
        in_specs=(
            P("seq", "chan"),
            P("seq", "chan"),
            P("seq", "chan"),
            P("chan"),
            P("chan"),
            P(),
            P(),
            P(),
            P(),
            P(None, "chan"),
        ),
        out_specs=(
            P("seq", "chan"),
            P("seq", "chan"),
            P("seq", "chan"),
            P("chan"),
            P(),
            P(),
            P(),
            P(),
            P(None, "chan"),
        ),
        check_vma=False,
    )
```

```python
import math

import jax
import jax.experimental.pallas as pl
import jax.experimental.pallas.tpu as pltpu
import jax.numpy as jnp
import ml_dtypes
import numpy as np
from jax import lax
from jax.sharding import PartitionSpec as P

BANDS = 16
ROWS = 256
PARTS = 128
HALF = 128
LENGTH = ROWS * PARTS
FULL = 2 * LENGTH
LIMIT = 64 << 20
FH = 64
EMB = 33

full_turn = 2.0 * math.pi
norm_eps = 1e-06
MESH = pl.DeviceIdType.MESH
BF = jnp.bfloat16
F32 = jnp.float32


def pieces(table):
    high = table.astype(ml_dtypes.bfloat16)
    low = (table - high.astype(np.float64)).astype(ml_dtypes.bfloat16)
    return high, low


def tables():
    freq = np.arange(HALF) + 0.5
    block = np.arange(PARTS)
    inner = np.arange(ROWS)
    outer_angle = full_turn * ((freq[:, None] * block[None, :]) % 256) / 256
    outer = np.concatenate([np.cos(outer_angle), -np.sin(outer_angle)], axis=0)
    back = outer.T * (2.0 / FULL)
    inner_angle = full_turn * ((inner[:, None] * inner[None, :]) % ROWS) / ROWS
    both = np.concatenate([np.cos(inner_angle), np.sin(inner_angle)], axis=1)
    twist = full_turn * (freq[:, None] * inner[None, :]) / FULL
    return (
        *pieces(outer),
        *pieces(back),
        *pieces(both),
        np.cos(twist).astype(np.float32),
        np.sin(twist).astype(np.float32),
    )


def split(arr):
    high = arr.astype(BF)
    return high, (arr - high.astype(F32)).astype(BF)


def dot(left, right):
    return jnp.dot(left, right, preferred_element_type=F32)


def dot3(left, right):
    return dot(left[0], right[0]) + dot(left[0], right[1]) + dot(left[1], right[0])


def contract(left, right, dims, precision):
    return lax.dot_general(
        left, right, ((dims[:1], dims[1:]), ((), ())), precision=precision, preferred_element_type=F32
    )


def total(arr):
    return jnp.sum(arr, axis=(0, 1), keepdims=True)


def deliver(*refs):
    count = len(refs) // 3
    heard, told = refs[-2:]
    ins, outs, held = refs[:count], refs[count : 2 * count], refs[2 * count : 3 * count]
    loads = [pltpu.make_async_copy(ins[at], held[at], heard.at[at]) for at in range(count)]
    stores = [pltpu.make_async_copy(held[at], outs[at], told.at[at]) for at in range(count)]
    for load in loads:
        load.start()
    for load, store in zip(loads, stores):
        load.wait()
        store.start()
    for store in stores:
        store.wait()


def kernel(
    signal_far,
    gating_far,
    cotangent_far,
    decay_far,
    skip_row_far,
    w1_far,
    b1_far,
    w2_far,
    b2_far,
    w3_far,
    outer_hi_far,
    outer_lo_far,
    back_hi_far,
    back_lo_far,
    both_hi_far,
    both_lo_far,
    twist_cos_far,
    twist_sin_far,
    output_far,
    grad_signal_far,
    grad_gating_far,
    grad_skip,
    grad_w1,
    grad_b1,
    grad_w2,
    grad_b2,
    grad_w3,
    output,
    grad_signal,
    grad_gating,
    store_sems,
    signal,
    gating,
    cotangent,
    decay,
    skip_row,
    w1,
    b1,
    w2,
    b2,
    w3,
    outer_hi,
    outer_lo,
    back_hi,
    back_lo,
    both_hi,
    both_lo,
    twist_cos,
    twist_sin,
    load_sems,
    w1s,
    w2s,
    emb,
    firstx,
    second,
    cos1,
    cos2,
    fade,
    wide,
    stage,
    send_a,
    recv_a,
    send_b,
    recv_b,
    send_c,
    recv_c,
    send_d,
    recv_d,
    send_e,
    recv_e,
    mid,
    mid_other,
    send_g,
    recv_g,
    send_f,
    recv_f,
    send_s,
    recv_s1,
    recv_s,
    shaped_keep,
    spec,
    vals,
    dfilt,
    send_sems,
    recv_sems,
):
    me = lax.axis_index("seq")
    core = lax.axis_index("chan")
    far = (
        signal_far,
        gating_far,
        cotangent_far,
        decay_far,
        skip_row_far,
        w1_far,
        b1_far,
        w2_far,
        b2_far,
        w3_far,
        outer_hi_far,
        outer_lo_far,
        back_hi_far,
        back_lo_far,
        both_hi_far,
        both_lo_far,
        twist_cos_far,
        twist_sin_far,
    )
    near = (
        signal,
        gating,
        cotangent,
        decay,
        skip_row,
        w1,
        b1,
        w2,
        b2,
        w3,
        outer_hi,
        outer_lo,
        back_hi,
        back_lo,
        both_hi,
        both_lo,
        twist_cos,
        twist_sin,
    )
    loads = [
        pltpu.make_async_copy(far[at], near[at], load_sems.at[at]) for at in range(len(far))
    ]

    depth = me >> 4
    plane_at = me & 15
    mine = (plane_at << 3) + depth
    barrier = pltpu.get_barrier_semaphore()

    far_half, near_half = (4, 3, 5, 2), (6, 1, 7, 0)

    def each(steps, visit):
        for ahead in steps:
            base = ((depth + ahead) & 7) << 4

            @pl.loop(1 if ahead == 0 else 0, 16)
            def _(step):
                visit(base + ((plane_at + (step if ahead == 0 else 10 + step)) & 15))

    def greet(dst):
        pl.semaphore_signal(barrier, inc=1, device_id={"seq": dst}, device_id_type=MESH)

    each(far_half + near_half, greet)
    pl.semaphore_signal(barrier, inc=1, device_id={"chan": 1 - core}, device_id_type=MESH)
    for load in loads:
        load.start()

    def push(src, dst, at, device):
        pltpu.make_async_remote_copy(
            src_ref=src,
            dst_ref=dst,
            send_sem=send_sems.at[at],
            recv_sem=recv_sems.at[at],
            device_id=device,
            device_id_type=MESH,
        ).start()

    def keep(src, dst, at):
        pltpu.make_async_copy(src, dst, recv_sems.at[at]).start()

    def inward(send, recv, at):
        def visit(dst):
            push(send.at[((dst & 15) << 3) + (dst >> 4)], recv.at[me], at, {"seq": dst})

        each(far_half + near_half, visit)
        keep(send.at[mine], recv.at[me], at)

    def outward(send, recv, at, steps):
        each(steps, lambda dst: push(send.at[dst], recv.at[mine], at, {"seq": dst}))
        if 0 in steps:
            keep(send.at[me], recv.at[mine], at)

    def over_depth(src_of, dst, at):
        for ahead in (4, 3, 5, 2, 6, 1, 7):
            peer = (depth + ahead) & 7
            push(src_of(peer), dst, at, {"seq": (peer << 4) + plane_at})
        keep(src_of(depth), dst, at)

    def over_plane(src_of, dst, at):
        for ahead in (2, 1, 3, 0):
            base = (((plane_at >> 2) + ahead) & 3) << 2

            @pl.loop(1 if ahead == 0 else 0, 4)
            def _(step):
                peer = base + ((plane_at + (step if ahead == 0 else 2 + step)) & 3)
                push(src_of(peer), dst, at, {"seq": (depth << 4) + peer})

        keep(src_of(plane_at), dst, at)

    def arrived(recv, at):
        pltpu.make_async_copy(recv, recv, recv_sems.at[at]).wait()

    def left(like, at, count=PARTS - 1):
        rest = like.at[pl.ds(0, count)]
        pltpu.make_async_copy(rest, rest, send_sems.at[at]).wait()

    def place(plane, arr):
        for q in range(2):
            for h in range(2):
                stage[:, 2 * q + h, plane * 128 : plane * 128 + 128] = arr[
                    q * 128 : q * 128 + 128, h * 128 : h * 128 + 128
                ]

    def put(plane, q, arr):
        for h in range(2):
            stage[:, 2 * q + h, plane * 128 : plane * 128 + 128] = arr[:, h * 128 : h * 128 + 128]

    def take(plane, q):
        return jnp.concatenate(
            [stage[:, 2 * q + h, plane * 128 : plane * 128 + 128] for h in range(2)], axis=1
        )

    for load in loads[:3]:
        load.wait()

    place(0, signal[...].astype(F32).T)
    dmixed_rows = cotangent[...].astype(F32) * gating[...].astype(F32)
    wide[...] = dmixed_rows.T
    high = wide[...].astype(BF).astype(F32)
    place(1, high)
    place(2, wide[...] - high)
    send_a[...] = stage[...].astype(BF)
    pl.semaphore_wait(barrier, PARTS)
    inward(send_a, recv_a, 0)

    for load in loads[3:]:
        load.wait()
    stamp = me * ROWS + lax.broadcasted_iota(jnp.int32, (BANDS, ROWS), 1)
    band = lax.broadcasted_iota(jnp.int32, (BANDS, ROWS), 0) + 1
    phase = ((stamp * band) & (LENGTH - 1)).astype(F32) * (full_turn / LENGTH)
    emb[0:16, :] = jnp.cos(phase)
    emb[16:32, :] = jnp.sin(phase)
    line = lax.broadcasted_iota(jnp.int32, (8, ROWS), 0)
    ramp = stamp[0:8].astype(F32)
    emb[32:40, :] = jnp.where(line == 0, ramp / LENGTH, jnp.where(line == 1, 1.0, 0.0))
    w1s[0:32, :] = w1[1:33, :]
    w1s[32:40, :] = jnp.zeros((8, FH), F32)
    w1s[32:33, :] = w1[0:1, :]
    w1s[33:34, :] = b1[...]
    w2s[0:64, :] = w2[...]
    w2s[64:72, :] = jnp.zeros((8, FH), F32)
    w2s[64:65, :] = b2[...]
    pre1 = contract(w1s[...], emb[...], (0, 0), lax.Precision.HIGHEST)
    firstx[0:64, :] = jnp.sin(pre1)
    firstx[64:72, :] = jnp.where(line == 0, 1.0, 0.0)
    cos1[...] = jnp.cos(pre1)
    pre2 = contract(w2s[...], firstx[...], (0, 0), lax.Precision.HIGHEST)
    second[...] = jnp.sin(pre2)
    cos2[...] = jnp.cos(pre2)
    rates = jnp.broadcast_to(decay[...], (ROWS, ROWS)).T
    fade[...] = jnp.exp(-jnp.broadcast_to(ramp[0:1], (ROWS, ROWS)) * rates)
    shaped_keep[...] = contract(w3[...], second[...], (0, 0), lax.Precision.HIGHEST) * fade[...]
    high = shaped_keep[...].astype(BF).astype(F32)
    place(0, high)
    place(1, shaped_keep[...] - high)
    send_b[...] = stage[:, :, 0:256].astype(BF)
    inward(send_b, recv_b, 1)

    both = (both_hi, both_lo)

    def forward(slot, parts):
        if len(parts) == 1:
            rows = dot(outer_hi[...], parts[0]) + dot(outer_lo[...], parts[0])
        else:
            rows = dot3((outer_hi[...], outer_lo[...]), parts)
        real, imag = rows[0:HALF], rows[HALF:]
        turned = jnp.concatenate(
            [
                real * twist_cos[...] + imag * twist_sin[...],
                imag * twist_cos[...] - real * twist_sin[...],
            ],
            axis=0,
        )
        out = dot3(split(turned), (both_hi[...], both_lo[...]))
        spec[slot, 0] = out[0:HALF, 0:ROWS] + out[HALF:, ROWS:]
        spec[slot, 1] = out[HALF:, 0:ROWS] - out[0:HALF, ROWS:]

    def inverse(real, imag):
        out = dot3(split(jnp.concatenate([real, imag], axis=0)), (both_hi[...], both_lo[...]))
        mid_real = out[0:HALF, 0:ROWS] - out[HALF:, ROWS:]
        mid_imag = out[HALF:, 0:ROWS] + out[0:HALF, ROWS:]
        turned = jnp.concatenate(
            [
                mid_real * twist_cos[...] - mid_imag * twist_sin[...],
                mid_imag * twist_cos[...] + mid_real * twist_sin[...],
            ],
            axis=0,
        )
        return dot3((back_hi[...], back_lo[...]), split(turned))

    arrived(recv_a, 0)
    stage[...] = recv_a[...].astype(F32)
    skip_grads = []
    channel = lax.broadcasted_iota(jnp.int32, (1, ROWS), 1)
    skips = [
        total(jnp.where(channel == mine + q * PARTS, skip_row[...], 0.0)) for q in range(2)
    ]
    for q in range(2):
        sig = take(0, q)
        high, low = take(1, q), take(2, q)
        vals[q] = high + low
        skip_grads.append(total(vals[q] * sig))
        forward(q, (sig.astype(BF),))
        forward(2 + q, (high.astype(BF), low.astype(BF)))
    for q in range(2):
        sig_re, sig_im, dm_re, dm_im = spec[q, 0], spec[q, 1], spec[2 + q, 0], spec[2 + q, 1]
        dfilt[q] = inverse(sig_re * dm_re + sig_im * dm_im, sig_re * dm_im - sig_im * dm_re)

    for q in range(2):
        high = dfilt[q].astype(BF).astype(F32)
        put(0, q, high)
        put(1, q, dfilt[q] - high)
    send_c[...] = stage[:, :, 0:256].astype(BF)
    outward(send_c, recv_c, 2, far_half)

    arrived(recv_b, 1)
    stage[:, :, 0:256] = recv_b[...].astype(F32)
    lane = lax.broadcasted_iota(jnp.int32, (1, 128), 1)
    filters, scales = [], []
    scalars = jnp.zeros((1, 128), F32)
    for q in range(2):
        high, low = take(0, q), take(1, q)
        shaped = high + low
        along = total(shaped * dfilt[q])
        scale = 1.0 / jnp.sqrt(total(shaped * shaped) + norm_eps)
        pull = along * scale * scale * scale
        filters.append((high.astype(BF), low.astype(BF)))
        scales.append(scale)
        scalars = jnp.where(lane == 2 * q, scale, jnp.where(lane == 2 * q + 1, pull, scalars))
    send_s[...] = scalars
    over_depth(lambda peer: send_s, recv_s1.at[depth], 7)
    outward(send_c, recv_c, 2, near_half)

    for q in range(2):
        forward(4 + q, filters[q])
    for q in range(2):
        filt_re, filt_im = spec[4 + q, 0] * scales[q], spec[4 + q, 1] * scales[q]
        sig_re, sig_im, dm_re, dm_im = spec[q, 0], spec[q, 1], spec[2 + q, 0], spec[2 + q, 1]
        conv = inverse(sig_re * filt_re - sig_im * filt_im, sig_re * filt_im + sig_im * filt_re)
        high = conv.astype(BF).astype(F32)
        put(0, q, high)
        put(1, q, conv - high)
        corr = inverse(filt_re * dm_re + filt_im * dm_im, filt_re * dm_im - filt_im * dm_re)
        put(2, q, corr + skips[q] * vals[q])
    send_d[...] = stage[...].astype(BF)
    arrived(recv_s1, 7)
    over_plane(lambda peer: recv_s1, recv_s.at[pl.ds(plane_at * 8, 8)], 8)
    outward(send_d, recv_d, 3, far_half)

    arrived(recv_c, 2)
    stage[:, :, 0:256] = recv_c[...].astype(F32)
    for q in range(2):
        at = pl.ds(q * 128, 128)
        wide[at, :] = (take(0, q) + take(1, q)) * fade[at, :]
    shaped_keep[...] = shaped_keep[...] * fade[...]
    arrived(recv_s, 8)
    factors = recv_s[:, 0, :]
    for q in range(2):
        at = pl.ds(q * 128, 128)
        scale, pull = factors[:, 2 * q : 2 * q + 1], factors[:, 2 * q + 1 : 2 * q + 2]
        wide[at, :] = wide[at, :] * scale - shaped_keep[at, :] * pull
    draw = wide[...]
    third = contract(draw, second[...], (1, 1), lax.Precision.HIGH)
    dpre2 = contract(w3[...], draw, (1, 0), lax.Precision.HIGH) * cos2[...]
    grad2 = contract(firstx[...], dpre2, (1, 1), lax.Precision.HIGH)
    dpre1 = contract(w2[...], dpre2, (1, 0), lax.Precision.HIGH) * cos1[...]
    grad1 = contract(emb[...], dpre1, (1, 1), lax.Precision.HIGH)
    send_e[:, 0, :] = jnp.concatenate([third[0:128], third[128:256]], axis=1)
    shared = jnp.concatenate([grad1, grad2, jnp.zeros((16, FH), F32)], axis=0)
    send_e[:, 1, :] = jnp.concatenate([shared, jnp.zeros((128, FH), F32)], axis=1)
    over_plane(lambda peer: send_e.at[pl.ds(peer * 8, 8)], recv_e.at[plane_at], 4)
    outward(send_d, recv_d, 3, near_half)
    arrived(recv_e, 4)
    part = jnp.sum(recv_e[...], axis=0)
    mid[...] = part
    push(mid, mid_other, 5, {"chan": 1 - core})
    owner = lax.broadcasted_iota(jnp.int32, (8, 2, 128), 0)
    row = lax.broadcasted_iota(jnp.int32, (8, 2, 128), 1)
    column = lax.broadcasted_iota(jnp.int32, (8, 2, 128), 2)
    here = (owner == depth) & (row == 1)
    extra = jnp.where(
        here & (column == FH),
        skip_grads[0][None],
        jnp.where(here & (column == FH + 1), skip_grads[1][None], 0.0),
    )
    arrived(mid_other, 5)
    both_cores = (row == 1) & (column < FH)
    send_g[...] = part + jnp.where(both_cores, mid_other[...], extra)
    over_depth(lambda peer: send_g, recv_g.at[depth], 6)
    arrived(recv_g, 6)
    send_f[...] = jnp.sum(recv_g[...], axis=0)
    over_plane(lambda peer: send_f, recv_f.at[pl.ds(plane_at * 8, 8)], 10)

    arrived(recv_d, 3)
    stage[...] = recv_d[...].astype(F32)
    for q in range(2):
        wide[q * 128 : q * 128 + 128, :] = take(0, q) + take(1, q)
    mixed = wide[...].T + skip_row[...] * signal[...].astype(F32)
    output[...] = (gating[...].astype(F32) * mixed).astype(BF)
    grad_gating[...] = (cotangent[...].astype(F32) * mixed).astype(BF)
    for q in range(2):
        wide[q * 128 : q * 128 + 128, :] = take(2, q)
    grad_signal[...] = wide[...].T.astype(BF)

    stores = [
        pltpu.make_async_copy(output, output_far, store_sems.at[0]),
        pltpu.make_async_copy(grad_signal, grad_signal_far, store_sems.at[1]),
        pltpu.make_async_copy(grad_gating, grad_gating_far, store_sems.at[2]),
    ]
    for store in stores:
        store.start()
    arrived(recv_f, 10)
    thirds = recv_f[:, 0, :].T
    grad_w3[:, 0:128] = thirds[0:64]
    grad_w3[:, 128:256] = thirds[64:128]
    rest = recv_f[:, 1, :]
    turned = rest.T
    grad_skip[:, 0:128] = turned[64:65]
    grad_skip[:, 128:256] = turned[65:66]
    grad_w1[1:33, :] = rest[0:32, 0:64]
    grad_w1[0:1, :] = rest[32:33, 0:64]
    grad_b1[...] = rest[33:34, 0:64]
    grad_w2[...] = rest[40:104, 0:64]
    grad_b2[...] = rest[104:105, 0:64]

    for store in stores:
        store.wait()
    left(send_a, 0)
    left(send_b, 1)
    left(send_c, 2)
    left(send_d, 3)
    left(send_e, 4, 120)
    left(mid, 5, 8)
    left(recv_g, 6, 7)
    left(recv_s1, 7, 7)
    left(recv_s, 8, 120)
    left(recv_f, 10, 120)


def body(
    signal,
    gating,
    cotangent,
    decay_rates,
    skip_gain,
    first_weight,
    first_bias,
    second_weight,
    second_bias,
    third_weight,
):
    vmem = pl.BlockSpec(memory_space=pltpu.VMEM)
    hbm = pl.BlockSpec(memory_space=pltpu.HBM)
    operands = (
        signal,
        gating,
        cotangent,
        decay_rates.reshape(1, ROWS),
        skip_gain.reshape(1, ROWS),
        first_weight,
        first_bias.reshape(1, FH),
        second_weight,
        second_bias.reshape(1, FH),
        third_weight,
        *[jnp.asarray(t) for t in tables()],
    )
    wide_msg = pltpu.VMEM((PARTS, 4, 384), BF)
    thin_msg = pltpu.VMEM((PARTS, 4, 256), BF)
    results = pl.pallas_call(
        kernel,
        out_shape=[
            jax.ShapeDtypeStruct((ROWS, ROWS), BF),
            jax.ShapeDtypeStruct((ROWS, ROWS), BF),
            jax.ShapeDtypeStruct((ROWS, ROWS), BF),
            jax.ShapeDtypeStruct((1, ROWS), F32),
            jax.ShapeDtypeStruct((EMB, FH), F32),
            jax.ShapeDtypeStruct((1, FH), F32),
            jax.ShapeDtypeStruct((FH, FH), F32),
            jax.ShapeDtypeStruct((1, FH), F32),
            jax.ShapeDtypeStruct((FH, ROWS), F32),
        ],
        in_specs=[hbm] * 18,
        out_specs=[hbm] * 3 + [vmem] * 6,
        scratch_shapes=[pltpu.VMEM((ROWS, ROWS), BF)] * 3
        + [pltpu.SemaphoreType.DMA((3,))]
        + [pltpu.VMEM(o.shape, o.dtype) for o in operands]
        + [
            pltpu.SemaphoreType.DMA((len(operands),)),
            pltpu.VMEM((40, FH), F32),
            pltpu.VMEM((72, FH), F32),
            pltpu.VMEM((40, ROWS), F32),
            pltpu.VMEM((72, ROWS), F32),
            pltpu.VMEM((FH, ROWS), F32),
            pltpu.VMEM((FH, ROWS), F32),
            pltpu.VMEM((FH, ROWS), F32),
            pltpu.VMEM((ROWS, ROWS), F32),
            pltpu.VMEM((ROWS, ROWS), F32),
            pltpu.VMEM((PARTS, 4, 384), F32),
            wide_msg,
            wide_msg,
            thin_msg,
            thin_msg,
            thin_msg,
            thin_msg,
            wide_msg,
            wide_msg,
            pltpu.VMEM((PARTS, 2, 128), F32),
            pltpu.VMEM((16, 8, 2, 128), F32),
            pltpu.VMEM((8, 2, 128), F32),
            pltpu.VMEM((8, 2, 128), F32),
            pltpu.VMEM((8, 2, 128), F32),
            pltpu.VMEM((8, 8, 2, 128), F32),
            pltpu.VMEM((8, 2, 128), F32),
            pltpu.VMEM((PARTS, 2, 128), F32),
            pltpu.VMEM((1, 128), F32),
            pltpu.VMEM((8, 1, 128), F32),
            pltpu.VMEM((PARTS, 1, 128), F32),
            pltpu.VMEM((ROWS, ROWS), F32),
            pltpu.VMEM((6, 2, HALF, ROWS), F32),
            pltpu.VMEM((2, PARTS, ROWS), F32),
            pltpu.VMEM((2, PARTS, ROWS), F32),
            pltpu.SemaphoreType.DMA((11,)),
            pltpu.SemaphoreType.DMA((11,)),
        ],
        compiler_params=pltpu.CompilerParams(
            collective_id=0, has_side_effects=True, vmem_limit_bytes=LIMIT
        ),
        name="hyena",
    )(*operands)
    results = pl.pallas_call(
        deliver,
        out_shape=[jax.ShapeDtypeStruct(r.shape, r.dtype) for r in results],
        in_specs=[hbm] * 9,
        out_specs=[hbm] * 9,
        scratch_shapes=[pltpu.VMEM(r.shape, r.dtype) for r in results]
        + [pltpu.SemaphoreType.DMA((9,)), pltpu.SemaphoreType.DMA((9,))],
        compiler_params=pltpu.CompilerParams(vmem_limit_bytes=LIMIT),
        name="deliver",
    )(*results)
    out, g_sig, g_gate, g_skip, g_w1, g_b1, g_w2, g_b2, g_w3 = results
    return (
        out,
        g_sig,
        g_gate,
        g_skip.reshape(ROWS),
        g_w1,
        g_b1.reshape(FH),
        g_w2,
        g_b2.reshape(FH),
        g_w3,
    )


def solution(mesh):
    return jax.shard_map(
        body,
        mesh=mesh,
        in_specs=(
            P("seq", "chan"),
            P("seq", "chan"),
            P("seq", "chan"),
            P("chan"),
            P("chan"),
            P(),
            P(),
            P(),
            P(),
            P(None, "chan"),
        ),
        out_specs=(
            P("seq", "chan"),
            P("seq", "chan"),
            P("seq", "chan"),
            P("chan"),
            P(),
            P(),
            P(),
            P(),
            P(None, "chan"),
        ),
        check_vma=False,
    )
```
